256 devices in a mesh: ep: 64 (over y_hi, z, x), ctr: 4 (over y_lo, core).
Axes of the slice: x: 4, y: 4 (y_hi: 2, y_lo: 2; y = y_hi * 2 + y_lo), z: 8, core: 2. Of those that a mesh axis runs over, the one named last changes fastest.
Arguments:
- episodes: bfloat16 [96, 32768], P(None, 'ep'), may hold values from -10 to 10
- centers: bfloat16 [96, 65536], P(None, 'ctr'), may hold values from -10 to 10
- coeffs: float32 [32, 65536], P(None, ('ctr', 'ep')), may hold values from -6 to 6
- residual: float32 [32, 65536], P(None, ('ctr', 'ep')), may hold values from -6 to 6
- direction: float32 [32, 65536], P(None, ('ctr', 'ep')), may hold values from -6 to 6
Outputs:
- coeffs_next: float32 [32, 65536], P(None, ('ctr', 'ep'))
- residual_next: float32 [32, 65536], P(None, ('ctr', 'ep'))
- direction_next: float32 [32, 65536], P(None, ('ctr', 'ep'))
The draws below stay inside these ranges and needn't reach their ends.
All inputs are finite; a program needn't handle non-finite values.
Results may differ from the reference program's by a relative error of at most 0.00076.
Values may be sent and summed in bfloat16 or wider, within the bound.
No kernel may reach another device: no remote copies, remote signals or barrier semaphores. Data moves between devices by JAX's collectives and lax.ppermute only.
A program may use at most 64 MiB of HBM per device.

```python
import math
import jax
import jax.numpy as jnp
from jax import lax

F = 96
TGT = 32
EPISODES = 32768
CENTERS = 65536


def cluster_frame(key):
    cluster_count = 64
    mean_key, scale_key, width_key = jax.random.split(key, 3)
    means = jax.random.truncated_normal(mean_key, -3.0, 3.0, (F, cluster_count), jnp.float32)
    scales = jnp.exp(jax.random.uniform(scale_key, (F, 1), jnp.float32, math.log(0.15), math.log(1.5)))
    widths = jnp.exp(jax.random.uniform(width_key, (1, cluster_count), jnp.float32, math.log(0.8), math.log(1.3)))
    return (means, scales, widths)


def place_points(key, frame, count, noise):
    cluster_count = 64
    means, scales, widths = frame
    labels = jax.random.randint(jax.random.fold_in(key, 11), (count,), 0, cluster_count)
    centre_part = jnp.take(means, labels, axis=1)
    width_part = jnp.take(widths, labels, axis=1)
    return centre_part + width_part * scales * noise


def draw_episodes(key, part):
    frame = cluster_frame(key)
    key = jax.random.fold_in(key, 1)
    noise_key = jax.random.fold_in(key, 2)
    noise = jax.random.truncated_normal(noise_key, -3.0, 3.0, (F, EPISODES), jnp.float32)
    return place_points(key, frame, EPISODES, noise).astype(jnp.bfloat16)


def draw_centers(key, part):
    frame = cluster_frame(key)
    key = jax.random.fold_in(key, 2)
    noise_key = jax.random.fold_in(key, 3)
    noise = jax.random.truncated_normal(noise_key, -3.0, 3.0, (F, CENTERS), jnp.float32)
    return place_points(key, frame, CENTERS, noise).astype(jnp.bfloat16)


def steps_of(rng, dims, shards, low, high):
    def one(position, shards_of):
        steps = jax.random.uniform(jax.random.fold_in(jax.random.fold_in(rng, 6), position), (shards_of,), jnp.float32, low / len(shards), high / len(shards))
        return jnp.repeat(jnp.exp(steps), dims[position] // shards_of).reshape((-1,) + (1,) * (len(dims) - position - 1))

    gain = one(*shards[0])
    for cut in shards[1:]:
        gain = gain * one(*cut)
    return gain


def normal_values(stream_key, extent, scale, bound, shards=(), kind=jnp.bfloat16):
    array = scale * jax.random.normal(stream_key, extent, jnp.float32)
    if shards:
        array = array * steps_of(stream_key, extent, shards, -0.22, 0.18)
    return jnp.clip(array, -bound, bound).astype(kind)


def setup_inputs(seed: int = 0) -> dict:
    splits = jax.random.split(jax.random.key(seed), 6)
    episodes = draw_episodes(jax.random.fold_in(splits[5], 71), 0)
    centers = draw_centers(jax.random.fold_in(splits[5], 71), 0)
    coeffs = normal_values(splits[2], (TGT, CENTERS), 1.0, 6.0, ((1, 256),), jnp.float32)
    residual = normal_values(splits[3], (TGT, CENTERS), 1.0, 6.0, ((1, 256),), jnp.float32)
    direction = normal_values(splits[4], (TGT, CENTERS), 1.0, 6.0, ((1, 256),), jnp.float32)
    return dict(episodes=episodes, centers=centers, coeffs=coeffs, residual=residual, direction=direction)


def kernel_tile(left_feat, left_norms, right_feat, right_norms, sharpness):
    cross = lax.dot_general(left_feat, right_feat, (((0,), (0,)), ((), ())), preferred_element_type=jnp.float32)
    distance = left_norms[:, None] + right_norms[None, :] - 2.0 * cross
    return jnp.exp(-sharpness * distance).astype(jnp.bfloat16)


def reference(episodes, centers, coeffs, residual, direction):
    sharpness = 3.0 / F
    block = math.gcd(CENTERS, 2048)
    count = CENTERS // block
    ep_norms = jnp.sum(jnp.square(episodes.astype(jnp.float32)), axis=0)
    cen_norms = jnp.sum(jnp.square(centers.astype(jnp.float32)), axis=0)
    dir_half = direction.astype(jnp.bfloat16)
    block_ids = jnp.arange(count, dtype=jnp.int32)

    def forward(carry, block_idx):
        offset = (block_idx * block).astype(jnp.int32)
        cols = lax.dynamic_slice_in_dim(centers, offset, block, 1)
        col_norms = lax.dynamic_slice_in_dim(cen_norms, offset, block, 0)
        kernel = kernel_tile(episodes, ep_norms, cols, col_norms, sharpness)
        part = lax.dynamic_slice_in_dim(dir_half, offset, block, 1)
        return carry + lax.dot_general(part, kernel, (((1,), (1,)), ((), ())), preferred_element_type=jnp.float32), None

    row_vals, _ = lax.scan(forward, jnp.zeros((TGT, EPISODES), jnp.float32), block_ids)
    row_half = row_vals.astype(jnp.bfloat16)

    def backward(block_idx):
        offset = (block_idx * block).astype(jnp.int32)
        cols = lax.dynamic_slice_in_dim(centers, offset, block, 1)
        col_norms = lax.dynamic_slice_in_dim(cen_norms, offset, block, 0)
        kernel = kernel_tile(episodes, ep_norms, cols, col_norms, sharpness)
        return jnp.dot(row_half, kernel, preferred_element_type=jnp.float32)

    gram_cols = lax.map(backward, block_ids)
    gram_cols = jnp.transpose(gram_cols, (1, 0, 2)).reshape(TGT, CENTERS)
    applied = gram_cols + 1.0 * direction
    old_norm = jnp.sum(residual * residual, axis=1)
    curvature = jnp.sum(direction * applied, axis=1)
    step_size = old_norm / curvature
    coeffs_next = coeffs + step_size[:, None] * direction
    residual_next = residual - step_size[:, None] * applied
    new_norm = jnp.sum(residual_next * residual_next, axis=1)
    direction_next = residual_next + (new_norm / old_norm)[:, None] * direction
    return (coeffs_next, residual_next, direction_next)
```

```python
import jax
import jax.numpy as jnp
from jax import lax
from jax.experimental import pallas as pl
from jax.experimental.pallas import tpu as pltpu
from jax.sharding import Mesh, PartitionSpec as P

AXES = ("yh", "z", "x", "yl", "c")
SIZES = (2, 8, 4, 2, 2)
SIZE = dict(zip(AXES, SIZES))
EP = ("yh", "z", "x")
CTR = ("yl", "c")
SPLIT = ("yh", "z")
MERGED = tuple(a for a in EP if a not in SPLIT)
ROWS = MERGED + CTR

F = 96
DEPTH = 128
TGT = 32
PIECE = 256
ROWPIECE = 128
SHARP = 3.0 / F
F32 = jnp.float32
BF16 = jnp.bfloat16
VMEM = 48 * 1024 * 1024


def prod(axes):
    out = 1
    for a in axes:
        out *= SIZE[a]
    return out


N_SPLIT, N_MERGED, N_ROWS = prod(SPLIT), prod(MERGED), prod(ROWS)
N_EP = 512 * N_MERGED


def three(v):
    hi = v.astype(BF16).astype(F32)
    mid = (v - hi).astype(BF16).astype(F32)
    return hi, mid, v - hi - mid


def extra_rows(norm_parts, first, width):
    row = lax.broadcasted_iota(jnp.int32, (DEPTH - F, width), 0)
    out = jnp.where(row < 6, 1.0, 0.0).astype(F32)
    for k, part in enumerate(norm_parts):
        out = jnp.where(row == first + k, part, out)
    return out


def tile_kernel(blocks, eps_ref, cen_ref, out_ref, left):
    @pl.when(pl.program_id(0) == 0)
    def _():
        for m in range(N_MERGED):
            e = eps_ref[m].astype(F32)
            norm = jnp.sum(e * e, axis=0, keepdims=True)
            tall = jnp.concatenate([e * (2.0 * SHARP), extra_rows(three(-SHARP * norm), 0, 512)], axis=0)
            left[m * 512:(m + 1) * 512, :] = tall.T.astype(BF16)

    c = cen_ref[...].astype(F32)
    norm = jnp.sum(c * c, axis=0, keepdims=True)
    right = jnp.concatenate([cen_ref[...], extra_rows(three(-SHARP * norm), 3, PIECE).astype(BF16)], axis=0)
    for r in range(0, N_EP, 256):
        arg = jnp.dot(left[r:r + 256, :], right, preferred_element_type=F32)
        out_ref[0, r:r + 256, :] = jnp.exp(arg).astype(BF16)


def tiles(blocks, eps, centers):
    return pl.pallas_call(
        tile_kernel,
        grid_spec=pltpu.PrefetchScalarGridSpec(
            num_scalar_prefetch=1,
            grid=(N_SPLIT,),
            in_specs=[
                pl.BlockSpec((N_MERGED, F, 512), lambda i, b: (0, 0, 0)),
                pl.BlockSpec((F, PIECE), lambda i, b: (0, b[i])),
            ],
            out_specs=pl.BlockSpec((1, N_EP, PIECE), lambda i, b: (i, 0, 0)),
            scratch_shapes=[pltpu.VMEM((N_EP, DEPTH), BF16)],
        ),
        out_shape=jax.ShapeDtypeStruct((N_SPLIT, N_EP, PIECE), BF16),
        compiler_params=pltpu.CompilerParams(vmem_limit_bytes=VMEM),
        cost_estimate=pl.CostEstimate(
            flops=2 * DEPTH * 2 ** 23, bytes_accessed=2 ** 24, transcendentals=2 ** 23
        ),
    )(blocks, eps, centers)


def row_kernel(d_ref, k_ref, out_ref, total):
    i = pl.program_id(0)

    @pl.when(i == 0)
    def _():
        total[...] = jnp.zeros_like(total)

    total[...] += lax.dot_general(d_ref[0], k_ref[0], (((1,), (1,)), ((), ())), preferred_element_type=F32)

    @pl.when(i == N_SPLIT - 1)
    def _():
        for j in range(N_ROWS):
            out_ref[j] = total[:, j * ROWPIECE:(j + 1) * ROWPIECE]


def row_sums(dirs, kmat):
    return pl.pallas_call(
        row_kernel,
        grid=(N_SPLIT,),
        in_specs=[
            pl.BlockSpec((1, TGT, PIECE), lambda i: (i, 0, 0)),
            pl.BlockSpec((1, N_EP, PIECE), lambda i: (i, 0, 0)),
        ],
        out_specs=pl.BlockSpec((N_ROWS, TGT, ROWPIECE), lambda i: (0, 0, 0)),
        out_shape=jax.ShapeDtypeStruct((N_ROWS, TGT, ROWPIECE), F32),
        scratch_shapes=[pltpu.VMEM((TGT, N_EP), F32)],
        compiler_params=pltpu.CompilerParams(vmem_limit_bytes=VMEM),
        cost_estimate=pl.CostEstimate(flops=2 * TGT * 2 ** 23, bytes_accessed=2 ** 24, transcendentals=0),
    )(dirs, kmat)


def spread_kernel(parts_ref, out_ref):
    half = jnp.sum(parts_ref[...], axis=0).astype(BF16)
    for j in range(N_ROWS):
        out_ref[j] = half


def spread(parts):
    return pl.pallas_call(
        spread_kernel, out_shape=jax.ShapeDtypeStruct((N_ROWS, TGT, ROWPIECE), BF16)
    )(parts)


def column_kernel(rows_ref, k_ref, out_ref, half):
    @pl.when(pl.program_id(0) == 0)
    def _():
        for j in range(N_ROWS):
            half[:, j * ROWPIECE:(j + 1) * ROWPIECE] = rows_ref[j]

    out_ref[0] = jnp.dot(half[...], k_ref[0], preferred_element_type=F32)


def column_sums(rows, kmat):
    return pl.pallas_call(
        column_kernel,
        grid=(N_SPLIT,),
        in_specs=[
            pl.BlockSpec((N_ROWS, TGT, ROWPIECE), lambda i: (0, 0, 0)),
            pl.BlockSpec((1, N_EP, PIECE), lambda i: (i, 0, 0)),
        ],
        out_specs=pl.BlockSpec((1, TGT, PIECE), lambda i: (i, 0, 0)),
        out_shape=jax.ShapeDtypeStruct((N_SPLIT, TGT, PIECE), F32),
        scratch_shapes=[pltpu.VMEM((TGT, N_EP), BF16)],
        compiler_params=pltpu.CompilerParams(vmem_limit_bytes=VMEM),
        cost_estimate=pl.CostEstimate(flops=2 * TGT * 2 ** 23, bytes_accessed=2 ** 24, transcendentals=0),
    )(rows, kmat)


def apply_kernel(parts_ref, r_ref, d_ref, applied_ref, sums_ref):
    r, d = r_ref[...], d_ref[...]
    a = jnp.sum(parts_ref[...], axis=0) + 1.0 * d
    applied_ref[...] = a
    terms = [p[:, :128] + p[:, 128:] for p in (r * r, r * a, d * a, a * a)]
    line = jnp.sum(jnp.concatenate(terms, axis=0).T, axis=0, keepdims=True)
    sums_ref[...] = jnp.broadcast_to(line, sums_ref.shape)


def apply_and_sum(parts, residual, direction):
    return pl.pallas_call(
        apply_kernel,
        out_shape=(
            jax.ShapeDtypeStruct((TGT, PIECE), F32),
            jax.ShapeDtypeStruct((256, 4 * TGT), F32),
        ),
    )(parts, residual, direction)


def step_kernel(sums_ref, coeffs_ref, r_ref, d_ref, a_ref, co_ref, ro_ref, do_ref, step_ref, doubt_ref):
    total = jnp.sum(sums_ref[...], axis=0, keepdims=True)
    cols = jnp.broadcast_to(total, (128, 128)).T
    old, ra, curv, aa = (cols[k * TGT:(k + 1) * TGT] for k in range(4))
    step = old / curv
    grown = step * (step * aa)
    new = old - 2.0 * (step * ra) + grown
    beta = new / old
    doubt_ref[0, 0] = jnp.max(jnp.where(new < 0.01 * (old + grown), 1, 0))
    step_ref[...] = jnp.concatenate([step, old], axis=0)
    wide = lambda v: jnp.concatenate([v, v], axis=1)
    d = d_ref[...]
    co_ref[...] = coeffs_ref[...] + wide(step) * d
    res = r_ref[...] - wide(step) * a_ref[...]
    ro_ref[...] = res
    do_ref[...] = res + wide(beta) * d


def step_and_update(sums, coeffs, residual, direction, applied):
    piece = jax.ShapeDtypeStruct((TGT, PIECE), F32)
    return pl.pallas_call(
        step_kernel,
        out_shape=(
            piece, piece, piece,
            jax.ShapeDtypeStruct((2 * TGT, 128), F32),
            jax.ShapeDtypeStruct((1, 1), jnp.int32),
        ),
        out_specs=(
            pl.BlockSpec(memory_space=pltpu.VMEM),
            pl.BlockSpec(memory_space=pltpu.VMEM),
            pl.BlockSpec(memory_space=pltpu.VMEM),
            pl.BlockSpec(memory_space=pltpu.VMEM),
            pl.BlockSpec(memory_space=pltpu.SMEM),
        ),
    )(sums, coeffs, residual, direction, applied)


def exchange(x, axes):
    return lax.all_to_all(x, axes, 0, 0, tiled=False)


def shards(episodes, centers, coeffs, residual, direction):
    place = jnp.int32(0)
    for a in EP:
        pos = jnp.int32(0) if a in SPLIT else lax.axis_index(a)
        place = place * SIZE[a] + pos
    grid = jnp.zeros((1,), jnp.int32)
    for a in EP:
        step = jnp.arange(SIZE[a], dtype=jnp.int32) if a in SPLIT else jnp.zeros((1,), jnp.int32)
        grid = (grid[:, None] * SIZE[a] + step[None, :]).reshape(-1)
    blocks = place + grid

    dir_half = direction.astype(BF16)
    dirs = exchange(jnp.broadcast_to(dir_half, (N_SPLIT, TGT, PIECE)), SPLIT)
    eps = exchange(jnp.broadcast_to(episodes, (N_MERGED, F, 512)), MERGED)
    kmat = tiles(blocks, eps, centers)
    row_parts = exchange(row_sums(dirs, kmat), ROWS)
    rows = exchange(spread(row_parts), ROWS)
    parts = exchange(column_sums(rows, kmat), SPLIT)
    applied, sums = apply_and_sum(parts, residual, direction)
    sums = exchange(sums.reshape(256, 1, 4 * TGT), AXES).reshape(256, 4 * TGT)
    coeffs_next, residual_next, direction_next, step, doubt = step_and_update(
        sums, coeffs, residual, direction, applied
    )

    def summed(_):
        new = lax.psum(jnp.sum(residual_next * residual_next, axis=1), AXES)
        return residual_next + (new / step[TGT:, 0])[:, None] * direction

    direction_next = lax.cond(doubt[0, 0] > 0, summed, lambda _: direction_next, 0)
    return coeffs_next, residual_next, direction_next


def solution(mesh):
    fine = Mesh(mesh.devices.reshape(SIZES), AXES)
    piece = P(None, CTR + EP)
    return jax.shard_map(
        shards,
        mesh=fine,
        in_specs=(P(None, EP), P(None, CTR), piece, piece, piece),
        out_specs=(piece, piece, piece),
        check_vma=False,
    )
```

```python
import jax
import jax.numpy as jnp
from jax import lax
from jax.experimental import pallas as pl
from jax.experimental.pallas import tpu as pltpu
from jax.sharding import Mesh, PartitionSpec as P

AXES = ("yh", "zh", "zm", "zl", "x", "yl", "c")
SIZES = (2, 2, 2, 2, 4, 2, 2)
SIZE = dict(zip(AXES, SIZES))
EP = ("yh", "zh", "zm", "zl", "x")
CTR = ("yl", "c")
SPLIT = ("yh", "zh", "zm", "zl")
MERGED = tuple(a for a in EP if a not in SPLIT)
ROWS = MERGED + CTR

F = 96
DEPTH = 128
TGT = 32
PIECE = 256
ROWPIECE = 128
OWN = 512
SHARP = 3.0 / F
F32 = jnp.float32
BF16 = jnp.bfloat16
IN_VMEM = pl.BlockSpec(memory_space=pltpu.VMEM)
IN_SMEM = pl.BlockSpec(memory_space=pltpu.SMEM)


def prod(axes):
    out = 1
    for a in axes:
        out *= SIZE[a]
    return out


def places(axes):
    out = [0]
    for a in EP:
        out = [p * SIZE[a] + k for p in out for k in range(SIZE[a] if a in axes else 1)]
    return out


N_SPLIT, N_MERGED, N_ROWS = prod(SPLIT), prod(MERGED), prod(ROWS)
N_EP = OWN * N_MERGED
BLOCKS = places(SPLIT)


def params(mib):
    return pltpu.CompilerParams(vmem_limit_bytes=mib * 1024 * 1024)


def here(x):
    return pltpu.with_memory_space_constraint(x, pltpu.VMEM)


def exchange(x, axes):
    return here(lax.all_to_all(here(x), axes, 0, 0, tiled=False))


def three(v):
    hi = v.astype(BF16).astype(F32)
    mid = (v - hi).astype(BF16).astype(F32)
    return hi, mid, v - hi - mid


def extra_rows(norm_parts, first, width):
    row = lax.broadcasted_iota(jnp.int32, (DEPTH - F, width), 0)
    out = jnp.where(row < 6, 1.0, 0.0).astype(F32)
    for k, part in enumerate(norm_parts):
        out = jnp.where(row == first + k, part, out)
    return out


def copies_kernel(d_ref, out_ref):
    half = d_ref[...].astype(BF16)
    for i in range(N_SPLIT):
        out_ref[i] = half


def copies(direction):
    return pl.pallas_call(
        copies_kernel, out_shape=pltpu.VMEM((N_SPLIT, TGT, PIECE), BF16), compiler_params=params(4)
    )(direction)


UNROLL = 4


def tile_kernel(*refs):
    place_ref, slot_ref = refs[:2]
    eps_refs = refs[2:2 + N_MERGED]
    cen_ref, d_ref, k_ref, out_ref, left, cens, own, sems = refs[2 + N_MERGED:]

    def fetch(i):
        start = pl.multiple_of((place_ref[0] + BLOCKS[i]) * PIECE, PIECE)
        return pltpu.make_async_copy(cen_ref.at[:, pl.ds(start, PIECE)], cens.at[i], sems.at[i])

    mine = pltpu.make_async_copy(eps_refs[0], own, sems.at[N_SPLIT])
    mine.start()
    for i in range(N_SPLIT):
        fetch(i).start()
    for m in reversed(range(N_MERGED)):
        if m == 0:
            mine.wait()
        e = (eps_refs[m] if m else own)[...].astype(F32)
        norm = jnp.sum(e * e, axis=0, keepdims=True)
        tall = jnp.concatenate([e * (2.0 * SHARP), extra_rows(three(-SHARP * norm), 0, OWN)], axis=0)
        slot = pl.multiple_of((slot_ref[0] ^ m) * OWN, OWN)
        left[pl.ds(slot, OWN), :] = tall.T.astype(BF16)
    for i in range(N_SPLIT):
        fetch(i).wait()

    def block(i):
        c = cens[i].astype(F32)
        norm = jnp.sum(c * c, axis=0, keepdims=True)
        right = jnp.concatenate([cens[i], extra_rows(three(-SHARP * norm), 3, PIECE).astype(BF16)], axis=0)
        for r in range(0, N_EP, 256):
            arg = jnp.dot(left[r:r + 256, :], right, preferred_element_type=F32)
            k_ref[i, r:r + 256, :] = jnp.exp(arg).astype(BF16)

    def step(n, carry):
        for u in range(UNROLL):
            block(n * UNROLL + u)
        return carry

    lax.fori_loop(0, N_SPLIT // UNROLL, step, 0)

    for r in range(0, N_EP, 512):
        total = None
        for i in range(N_SPLIT):
            part = lax.dot_general(
                k_ref[i, r:r + 512, :], d_ref[i], (((1,), (1,)), ((), ())), preferred_element_type=F32
            )
            total = part if total is None else total + part
        total = total.T
        for j in range(512 // ROWPIECE):
            out_ref[r // ROWPIECE + j] = total[:, j * ROWPIECE:(j + 1) * ROWPIECE]


def tiles_and_rows(place, slot, eps, centers, dirs):
    in_hbm = lambda x: pltpu.with_memory_space_constraint(x, pltpu.HBM)
    anywhere = pl.BlockSpec(memory_space=pl.ANY)
    return pl.pallas_call(
        tile_kernel,
        in_specs=[IN_SMEM] * 2 + [anywhere] + [IN_VMEM] * (N_MERGED - 1) + [anywhere, IN_VMEM],
        out_specs=(IN_VMEM, IN_VMEM),
        out_shape=(pltpu.VMEM((N_SPLIT, N_EP, PIECE), BF16), pltpu.VMEM((N_ROWS, TGT, ROWPIECE), F32)),
        scratch_shapes=[
            pltpu.VMEM((N_EP, DEPTH), BF16),
            pltpu.VMEM((N_SPLIT, F, PIECE), BF16),
            pltpu.VMEM((F, OWN), BF16),
            pltpu.SemaphoreType.DMA((N_SPLIT + 1,)),
        ],
        compiler_params=params(24),
        cost_estimate=pl.CostEstimate(
            flops=2 * (DEPTH + TGT) * 2 ** 23, bytes_accessed=2 ** 24, transcendentals=2 ** 23
        ),
    )(place, slot, in_hbm(eps[0]), *eps[1:], in_hbm(centers), dirs)


def spread_kernel(parts_ref, out_ref):
    half = jnp.sum(parts_ref[...], axis=0).astype(BF16)
    for j in range(N_ROWS):
        out_ref[j] = half


def spread(parts):
    return pl.pallas_call(
        spread_kernel, out_shape=pltpu.VMEM((N_ROWS, TGT, ROWPIECE), BF16), compiler_params=params(4)
    )(parts)


def column_kernel(rows_ref, k_ref, out_ref, half):
    for j in range(N_ROWS):
        half[:, j * ROWPIECE:(j + 1) * ROWPIECE] = rows_ref[j]
    for i in range(N_SPLIT):
        out_ref[i] = jnp.dot(half[...], k_ref[i], preferred_element_type=F32)


def column_sums(rows, kmat):
    return pl.pallas_call(
        column_kernel,
        in_specs=[IN_VMEM] * 2,
        out_specs=IN_VMEM,
        out_shape=pltpu.VMEM((N_SPLIT, TGT, PIECE), F32),
        scratch_shapes=[pltpu.VMEM((TGT, N_EP), BF16)],
        compiler_params=params(8),
        cost_estimate=pl.CostEstimate(flops=2 * TGT * 2 ** 23, bytes_accessed=2 ** 24, transcendentals=0),
    )(rows, here(kmat))


def lane_sums(v):
    return jnp.broadcast_to(jnp.sum(v, axis=1, keepdims=True), (TGT, 128))


def wide(v):
    return jnp.concatenate([v, v], axis=1)


def apply_kernel(parts_ref, r_ref, d_ref, applied_ref, sums_ref):
    r, d = r_ref[...], d_ref[...]
    a = jnp.sum(parts_ref[...], axis=0) + 1.0 * d
    applied_ref[...] = a
    aa = lane_sums(a * a)
    fit = jnp.where(aa > 0.0, lane_sums(r * a) / jnp.where(aa > 0.0, aa, 1.0), 0.0)
    rest = r - wide(fit) * a
    cols = jnp.concatenate([lane_sums(rest * rest), fit, aa, lane_sums(d * a)], axis=0)
    sums_ref[...] = jnp.broadcast_to(cols.T[:1], sums_ref.shape)


def apply_and_sum(parts, residual, direction):
    return pl.pallas_call(
        apply_kernel,
        out_shape=(pltpu.VMEM((TGT, PIECE), F32), jax.ShapeDtypeStruct((256, 4 * TGT), F32)),
        compiler_params=params(4),
    )(parts, residual, direction)


def step_kernel(sums_ref, coeffs_ref, r_ref, d_ref, a_ref, co_ref, ro_ref, do_ref):
    rest, fit, aa, da = (sums_ref[:, k * TGT:(k + 1) * TGT] for k in range(4))
    old = jnp.sum(rest + fit * (fit * aa), axis=0, keepdims=True)
    step = old / jnp.sum(da, axis=0, keepdims=True)
    off = step - fit
    new = jnp.sum(rest + off * (off * aa), axis=0, keepdims=True)
    step = wide(jnp.broadcast_to(step, (128, TGT)).T)
    beta = wide(jnp.broadcast_to(new / old, (128, TGT)).T)
    d = d_ref[...]
    co_ref[...] = coeffs_ref[...] + step * d
    res = r_ref[...] - step * a_ref[...]
    ro_ref[...] = res
    do_ref[...] = res + beta * d


def step_and_update(sums, coeffs, residual, direction, applied):
    return pl.pallas_call(
        step_kernel,
        out_shape=(jax.ShapeDtypeStruct((TGT, PIECE), F32),) * 3,
        compiler_params=params(4),
    )(sums, coeffs, residual, direction, here(applied))


def swaps(x):
    pairs = lambda m: [(k, k ^ m) for k in range(N_MERGED)]
    return [x] + [lax.ppermute(x, MERGED, pairs(m)) for m in range(1, N_MERGED)]


def shards(episodes, centers, coeffs, residual, direction):
    place = jnp.int32(0)
    slot = jnp.int32(0)
    for a in EP:
        if a in SPLIT:
            place = place * SIZE[a]
        else:
            place = place * SIZE[a] + lax.axis_index(a)
            slot = slot * SIZE[a] + lax.axis_index(a)

    eps = swaps(episodes)
    dirs = exchange(copies(direction), SPLIT)
    kmat, row_parts = tiles_and_rows(place.reshape(1), slot.reshape(1), eps, centers, dirs)
    row_parts = exchange(row_parts, ROWS)
    rows = exchange(spread(row_parts), ROWS)
    parts = exchange(column_sums(rows, kmat), SPLIT)
    applied, sums = apply_and_sum(parts, residual, direction)
    sums = lax.all_to_all(sums.reshape(256, 1, 4 * TGT), AXES, 0, 0, tiled=False).reshape(256, 4 * TGT)
    return step_and_update(sums, coeffs, residual, direction, applied)


def solution(mesh):
    fine = Mesh(mesh.devices.reshape(SIZES), AXES)
    piece = P(None, CTR + EP)
    return jax.shard_map(
        shards,
        mesh=fine,
        in_specs=(P(None, EP), P(None, CTR), piece, piece, piece),
        out_specs=(piece, piece, piece),
        check_vma=False,
    )
```

```python
import functools

import jax
import jax.numpy as jnp
from jax import lax
from jax.experimental import pallas as pl
from jax.experimental.pallas import tpu as pltpu
from jax.sharding import Mesh, PartitionSpec as P

AXES = ("yh", "zh", "zm", "zl", "x", "yl", "c")
SIZES = (2, 2, 2, 2, 4, 2, 2)
SIZE = dict(zip(AXES, SIZES))
EP = ("yh", "zh", "zm", "zl", "x")
CTR = ("yl", "c")
SPLIT = ("yh", "zh", "zm", "zl")
MERGED = tuple(a for a in EP if a not in SPLIT)
ROWS = MERGED + CTR

F = 96
DEPTH = 128
TGT = 32
PIECE = 256
ROWPIECE = 128
OWN = 512
SHARP = 3.0 / F
F32 = jnp.float32
BF16 = jnp.bfloat16
F16 = jnp.float16
IN_VMEM = pl.BlockSpec(memory_space=pltpu.VMEM)
IN_SMEM = pl.BlockSpec(memory_space=pltpu.SMEM)


def prod(axes):
    out = 1
    for a in axes:
        out *= SIZE[a]
    return out


def places(axes):
    out = [0]
    for a in EP:
        out = [p * SIZE[a] + k for p in out for k in range(SIZE[a] if a in axes else 1)]
    return out


N_SPLIT, N_MERGED, N_ROWS = prod(SPLIT), prod(MERGED), prod(ROWS)
N_EP = OWN * N_MERGED
BLOCKS = places(SPLIT)


def params(mib):
    return pltpu.CompilerParams(vmem_limit_bytes=mib * 1024 * 1024)


def here(x):
    return pltpu.with_memory_space_constraint(x, pltpu.VMEM)


def exchange(x, axes):
    return here(lax.all_to_all(here(x), axes, 0, 0, tiled=False))


def three(v):
    hi = v.astype(BF16).astype(F32)
    mid = (v - hi).astype(BF16).astype(F32)
    return hi, mid, v - hi - mid


def extra_rows(norm_parts, first, width):
    row = lax.broadcasted_iota(jnp.int32, (DEPTH - F, width), 0)
    out = jnp.where(row < 6, 1.0, 0.0).astype(F32)
    for k, part in enumerate(norm_parts):
        out = jnp.where(row == first + k, part, out)
    return out


def copies_kernel(d_ref, out_ref):
    half = d_ref[...].astype(BF16)
    for i in range(N_SPLIT):
        out_ref[i] = half


def copies(direction):
    return pl.pallas_call(
        copies_kernel, out_shape=pltpu.VMEM((N_SPLIT, TGT, PIECE), BF16), compiler_params=params(4)
    )(direction)


UNROLL = 4


def tile_kernel(*refs):
    place_ref, slot_ref = refs[:2]
    eps_refs = refs[2:2 + N_MERGED]
    cen_ref, d_ref, k_ref, out_ref, left, cens, own, sems = refs[2 + N_MERGED:]

    def fetch(i):
        start = pl.multiple_of((place_ref[0] + BLOCKS[i]) * PIECE, PIECE)
        return pltpu.make_async_copy(cen_ref.at[:, pl.ds(start, PIECE)], cens.at[i], sems.at[i])

    mine = pltpu.make_async_copy(eps_refs[0], own, sems.at[N_SPLIT])
    mine.start()
    for i in range(N_SPLIT):
        fetch(i).start()
    for m in reversed(range(N_MERGED)):
        if m == 0:
            mine.wait()
        e = (eps_refs[m] if m else own)[...].astype(F32)
        norm = jnp.sum(e * e, axis=0, keepdims=True)
        tall = jnp.concatenate([e * (2.0 * SHARP), extra_rows(three(-SHARP * norm), 0, OWN)], axis=0)
        slot = pl.multiple_of((slot_ref[0] ^ m) * OWN, OWN)
        left[pl.ds(slot, OWN), :] = tall.T.astype(BF16)
    for i in range(N_SPLIT):
        fetch(i).wait()

    def block(i):
        c = cens[i].astype(F32)
        norm = jnp.sum(c * c, axis=0, keepdims=True)
        right = jnp.concatenate([cens[i], extra_rows(three(-SHARP * norm), 3, PIECE).astype(BF16)], axis=0)
        for r in range(0, N_EP, 256):
            arg = jnp.dot(left[r:r + 256, :], right, preferred_element_type=F32)
            k_ref[i, r:r + 256, :] = jnp.exp(arg).astype(BF16)

    def step(n, carry):
        for u in range(UNROLL):
            block(n * UNROLL + u)
        return carry

    lax.fori_loop(0, N_SPLIT // UNROLL, step, 0)

    for r in range(0, N_EP, 512):
        total = None
        for i in range(N_SPLIT):
            part = lax.dot_general(
                k_ref[i, r:r + 512, :], d_ref[i], (((1,), (1,)), ((), ())), preferred_element_type=F32
            )
            total = part if total is None else total + part
        total = total.T
        for j in range(512 // ROWPIECE):
            out_ref[r // ROWPIECE + j] = total[:, j * ROWPIECE:(j + 1) * ROWPIECE]


def tiles_and_rows(place, slot, eps, centers, dirs):
    in_hbm = lambda x: pltpu.with_memory_space_constraint(x, pltpu.HBM)
    anywhere = pl.BlockSpec(memory_space=pl.ANY)
    return pl.pallas_call(
        tile_kernel,
        in_specs=[IN_SMEM] * 2 + [anywhere] + [IN_VMEM] * (N_MERGED - 1) + [anywhere, IN_VMEM],
        out_specs=(IN_VMEM, IN_VMEM),
        out_shape=(pltpu.VMEM((N_SPLIT, N_EP, PIECE), BF16), pltpu.VMEM((N_ROWS, TGT, ROWPIECE), F32)),
        scratch_shapes=[
            pltpu.VMEM((N_EP, DEPTH), BF16),
            pltpu.VMEM((N_SPLIT, F, PIECE), BF16),
            pltpu.VMEM((F, OWN), BF16),
            pltpu.SemaphoreType.DMA((N_SPLIT + 1,)),
        ],
        compiler_params=params(24),
        cost_estimate=pl.CostEstimate(
            flops=2 * (DEPTH + TGT) * 2 ** 23, bytes_accessed=2 ** 24, transcendentals=2 ** 23
        ),
    )(place, slot, in_hbm(eps[0]), *eps[1:], in_hbm(centers), dirs)


def spread_kernel(parts_ref, out_ref):
    half = jnp.sum(parts_ref[...], axis=0).astype(BF16)
    for j in range(N_ROWS):
        out_ref[j] = half


def spread(parts):
    return pl.pallas_call(
        spread_kernel, out_shape=pltpu.VMEM((N_ROWS, TGT, ROWPIECE), BF16), compiler_params=params(4)
    )(parts)


MESSAGE = 72
HALF = PIECE // 2


def column_kernel(rows_ref, k_ref, out_ref, half):
    for j in range(N_ROWS):
        half[:, j * ROWPIECE:(j + 1) * ROWPIECE] = rows_ref[j]
    sums = [jnp.dot(half[...], k_ref[i], preferred_element_type=F32) for i in range(N_SPLIT)]
    top = functools.reduce(jnp.maximum, [jnp.abs(v) for v in sums])
    top = jnp.max(jnp.maximum(top[:, :HALF], top[:, HALF:]), axis=1, keepdims=True)
    power = jnp.ceil(jnp.log2(jnp.maximum(jnp.broadcast_to(top, (TGT, HALF)), 1e-30)))
    scale = jnp.exp2(15.0 - power)
    line = jnp.concatenate([power] * (HALF // TGT), axis=0).T[:MESSAGE - 2 * TGT]
    for i in range(N_SPLIT):
        out_ref[i, :TGT, :] = sums[i][:, :HALF] * scale
        out_ref[i, TGT:2 * TGT, :] = sums[i][:, HALF:] * scale
        out_ref[i, 2 * TGT:, :] = line


def column_sums(rows, kmat):
    return pl.pallas_call(
        column_kernel,
        in_specs=[IN_VMEM] * 2,
        out_specs=IN_VMEM,
        out_shape=jax.ShapeDtypeStruct((N_SPLIT, MESSAGE, HALF), F32),
        scratch_shapes=[pltpu.VMEM((TGT, N_EP), BF16)],
        compiler_params=params(8),
        cost_estimate=pl.CostEstimate(flops=2 * TGT * 2 ** 23, bytes_accessed=2 ** 24, transcendentals=0),
    )(rows, here(kmat))


def gathered(parts_ref):
    low = high = 0.0
    for i in range(N_SPLIT):
        power = jnp.broadcast_to(parts_ref[i, 2 * TGT:2 * TGT + 1, :], (HALF, HALF)).T[:TGT]
        back = jnp.exp2(power - 15.0)
        low = low + parts_ref[i, :TGT, :] * back
        high = high + parts_ref[i, TGT:2 * TGT, :] * back
    return jnp.concatenate([low, high], axis=1)


def lane_sums(v):
    return jnp.broadcast_to(jnp.sum(v, axis=1, keepdims=True), (TGT, 128))


def wide(v):
    return jnp.concatenate([v, v], axis=1)


def apply_kernel(parts_ref, r_ref, d_ref, applied_ref, sums_ref):
    r, d = r_ref[...], d_ref[...]
    a = gathered(parts_ref) + 1.0 * d
    applied_ref[...] = a
    aa = lane_sums(a * a)
    fit = jnp.where(aa > 0.0, lane_sums(r * a) / jnp.where(aa > 0.0, aa, 1.0), 0.0)
    rest = r - wide(fit) * a
    cols = jnp.concatenate([lane_sums(rest * rest), fit, aa, lane_sums(d * a)], axis=0)
    sums_ref[...] = jnp.broadcast_to(cols.T[:1], sums_ref.shape)


def apply_and_sum(parts, residual, direction):
    return pl.pallas_call(
        apply_kernel,
        out_shape=(pltpu.VMEM((TGT, PIECE), F32), jax.ShapeDtypeStruct((256, 4 * TGT), F32)),
        compiler_params=params(4),
    )(parts, residual, direction)


def step_kernel(sums_ref, coeffs_ref, r_ref, d_ref, a_ref, co_ref, ro_ref, do_ref):
    rest, fit, aa, da = (sums_ref[:, k * TGT:(k + 1) * TGT] for k in range(4))
    old = jnp.sum(rest + fit * (fit * aa), axis=0, keepdims=True)
    step = old / jnp.sum(da, axis=0, keepdims=True)
    off = step - fit
    new = jnp.sum(rest + off * (off * aa), axis=0, keepdims=True)
    step = wide(jnp.broadcast_to(step, (128, TGT)).T)
    beta = wide(jnp.broadcast_to(new / old, (128, TGT)).T)
    d = d_ref[...]
    co_ref[...] = coeffs_ref[...] + step * d
    res = r_ref[...] - step * a_ref[...]
    ro_ref[...] = res
    do_ref[...] = res + beta * d


def step_and_update(sums, coeffs, residual, direction, applied):
    return pl.pallas_call(
        step_kernel,
        out_shape=(jax.ShapeDtypeStruct((TGT, PIECE), F32),) * 3,
        compiler_params=params(4),
    )(sums, coeffs, residual, direction, here(applied))


def swaps(x):
    pairs = lambda m: [(k, k ^ m) for k in range(N_MERGED)]
    return [x] + [lax.ppermute(x, MERGED, pairs(m)) for m in range(1, N_MERGED)]


def shards(episodes, centers, coeffs, residual, direction):
    place = jnp.int32(0)
    slot = jnp.int32(0)
    for a in EP:
        if a in SPLIT:
            place = place * SIZE[a]
        else:
            place = place * SIZE[a] + lax.axis_index(a)
            slot = slot * SIZE[a] + lax.axis_index(a)

    eps = swaps(episodes)
    dirs = exchange(copies(direction), SPLIT)
    kmat, row_parts = tiles_and_rows(place.reshape(1), slot.reshape(1), eps, centers, dirs)
    row_parts = exchange(row_parts, ROWS)
    rows = exchange(spread(row_parts), ROWS)
    parts = column_sums(rows, kmat).astype(F16)
    parts = lax.all_to_all(parts, SPLIT, 0, 0, tiled=False).astype(F32)
    applied, sums = apply_and_sum(parts, residual, direction)
    sums = lax.all_to_all(sums.reshape(256, 1, 4 * TGT), AXES, 0, 0, tiled=False).reshape(256, 4 * TGT)
    return step_and_update(sums, coeffs, residual, direction, applied)


def solution(mesh):
    fine = Mesh(mesh.devices.reshape(SIZES), AXES)
    piece = P(None, CTR + EP)
    return jax.shard_map(
        shards,
        mesh=fine,
        in_specs=(P(None, EP), P(None, CTR), piece, piece, piece),
        out_specs=(piece, piece, piece),
        check_vma=False,
    )
```

```python
import functools

import jax
import jax.numpy as jnp
from jax import lax
from jax.experimental import pallas as pl
from jax.experimental.pallas import tpu as pltpu
from jax.sharding import Mesh, PartitionSpec as P

AXES = ("yh", "z", "x", "yl", "c")
SIZES = (2, 8, 4, 2, 2)
EP = ("yh", "z", "x")
CTR = ("yl", "c")
SPLIT = ("yh", "z")
ROWS = ("x", "yl", "c")
N_SPLIT, N_X, N_ROWS = 16, 4, 16

F = 96
DEPTH = 128
TGT = 32
PIECE = 256
ROWPIECE = 128
OWN = 512
PER = OWN // ROWPIECE
N_EP = N_X * OWN
EARLY = 2 * OWN
SHARP = 3.0 / F
F32 = jnp.float32
BF16 = jnp.bfloat16
F16 = jnp.float16
IN_VMEM = pl.BlockSpec(memory_space=pltpu.VMEM)
IN_SMEM = pl.BlockSpec(memory_space=pltpu.SMEM)
ANYWHERE = pl.BlockSpec(memory_space=pl.ANY)


def params(mib):
    return pltpu.CompilerParams(vmem_limit_bytes=mib * 1024 * 1024)


def here(x):
    return pltpu.with_memory_space_constraint(x, pltpu.VMEM)


def in_hbm(x):
    return pltpu.with_memory_space_constraint(x, pltpu.HBM)


def exchange(x, axes):
    return here(lax.all_to_all(here(x), axes, 0, 0, tiled=False))


def three(v):
    hi = v.astype(BF16).astype(F32)
    mid = (v - hi).astype(BF16).astype(F32)
    return hi, mid, v - hi - mid


def extra_rows(norm_parts, first, width):
    row = lax.broadcasted_iota(jnp.int32, (DEPTH - F, width), 0)
    out = jnp.where(row < 6, 1.0, 0.0).astype(F32)
    for k, part in enumerate(norm_parts):
        out = jnp.where(row == first + k, part, out)
    return out


def copies_kernel(d_ref, out_ref, mine, sem):
    load = pltpu.make_async_copy(d_ref, mine, sem)
    load.start()
    load.wait()
    half = mine[...].astype(BF16)
    for i in range(N_SPLIT):
        out_ref[i] = half


def copies(direction):
    return pl.pallas_call(
        copies_kernel,
        in_specs=[ANYWHERE],
        out_specs=IN_VMEM,
        out_shape=pltpu.VMEM((N_SPLIT, TGT, PIECE), BF16),
        scratch_shapes=[pltpu.VMEM((TGT, PIECE), F32), pltpu.SemaphoreType.DMA],
        compiler_params=params(4),
    )(in_hbm(direction))


def left_block(e):
    e = e.astype(F32)
    norm = jnp.sum(e * e, axis=0, keepdims=True)
    tall = jnp.concatenate([e * (2.0 * SHARP), extra_rows(three(-SHARP * norm), 0, OWN)], axis=0)
    return tall.T.astype(BF16)


def tile(left, right):
    return jnp.exp(jnp.dot(left, right, preferred_element_type=F32)).astype(BF16)


def early_kernel(place_ref, own_ref, next_ref, cen_ref, k_ref, right_ref, left, own, cens, ready, cen_sems, own_sem,
                 out_sems):
    def fetch(i):
        start = pl.multiple_of((place_ref[0] + i * N_X) * PIECE, PIECE)
        return pltpu.make_async_copy(cen_ref.at[:, pl.ds(start, PIECE)], cens.at[i], cen_sems.at[i])

    def store(i):
        return pltpu.make_async_copy(ready.at[i], k_ref.at[i], out_sems.at[i])

    mine = pltpu.make_async_copy(own_ref, own, own_sem)
    mine.start()
    for i in range(N_SPLIT):
        fetch(i).start()
    left[OWN:, :] = left_block(next_ref[...])
    mine.wait()
    left[:OWN, :] = left_block(own[...])
    for i in range(N_SPLIT):
        fetch(i).wait()
    for i in range(N_SPLIT):
        c = cens[i].astype(F32)
        norm = jnp.sum(c * c, axis=0, keepdims=True)
        right = jnp.concatenate([cens[i], extra_rows(three(-SHARP * norm), 3, PIECE).astype(BF16)], axis=0)
        right_ref[i] = right
        for r in range(0, EARLY, 256):
            ready[i, r:r + 256, :] = tile(left[r:r + 256, :], right)
        store(i).start()
    for i in range(N_SPLIT):
        store(i).wait()


def early_tiles(place, own, near, centers):
    return pl.pallas_call(
        early_kernel,
        in_specs=[IN_SMEM, ANYWHERE, IN_VMEM, ANYWHERE],
        out_specs=(ANYWHERE, IN_VMEM),
        out_shape=(
            pltpu.HBM((N_SPLIT, EARLY, PIECE), BF16),
            jax.ShapeDtypeStruct((N_SPLIT, DEPTH, PIECE), BF16),
        ),
        scratch_shapes=[
            pltpu.VMEM((EARLY, DEPTH), BF16),
            pltpu.VMEM((F, OWN), BF16),
            pltpu.VMEM((N_SPLIT, F, PIECE), BF16),
            pltpu.VMEM((N_SPLIT, EARLY, PIECE), BF16),
            pltpu.SemaphoreType.DMA((N_SPLIT,)),
            pltpu.SemaphoreType.DMA,
            pltpu.SemaphoreType.DMA((N_SPLIT,)),
        ],
        compiler_params=params(20),
        cost_estimate=pl.CostEstimate(flops=10 ** 11, bytes_accessed=2 ** 23, transcendentals=2 ** 22),
    )(place, in_hbm(own), near, in_hbm(centers))


def late_kernel(x_ref, p2_ref, p3_ref, right_ref, early_ref, d_ref, k_ref, out_ref, left, sem):
    load = pltpu.make_async_copy(early_ref, k_ref.at[:, pl.ds(0, EARLY), :], sem)
    load.start()
    for m, ref in enumerate((p2_ref, p3_ref)):
        left[m * OWN:(m + 1) * OWN, :] = left_block(ref[...])
    for i in range(N_SPLIT):
        for r in range(0, N_EP - EARLY, 256):
            k_ref[i, EARLY + r:EARLY + r + 256, :] = tile(left[r:r + 256, :], right_ref[i])
    for m in (2, 3, 0, 1):
        if m == 0:
            load.wait()
        total = None
        for i in range(N_SPLIT):
            part = lax.dot_general(
                k_ref[i, m * OWN:(m + 1) * OWN, :], d_ref[i], (((1,), (1,)), ((), ())), preferred_element_type=F32
            )
            total = part if total is None else total + part
        total = total.T
        for q in range(PER):
            out_ref[(x_ref[0] ^ m) * PER + q] = total[:, q * ROWPIECE:(q + 1) * ROWPIECE]


def tiles_and_rows(x, far, right, early, dirs):
    return pl.pallas_call(
        late_kernel,
        in_specs=[IN_SMEM] + [IN_VMEM] * 3 + [ANYWHERE, IN_VMEM],
        out_specs=(IN_VMEM,) * 2,
        out_shape=(
            pltpu.VMEM((N_SPLIT, N_EP, PIECE), BF16),
            pltpu.VMEM((N_ROWS, TGT, ROWPIECE), F32),
        ),
        scratch_shapes=[pltpu.VMEM((N_EP - EARLY, DEPTH), BF16), pltpu.SemaphoreType.DMA],
        compiler_params=params(16),
        cost_estimate=pl.CostEstimate(
            flops=2 * (DEPTH + TGT) * 2 ** 23, bytes_accessed=2 ** 24, transcendentals=2 ** 23
        ),
    )(x, *far, right, in_hbm(early), dirs)


def spread_kernel(parts_ref, out_ref):
    half = jnp.sum(parts_ref[...], axis=0).astype(BF16)
    for j in range(N_ROWS):
        out_ref[j] = half


def spread(parts):
    return pl.pallas_call(
        spread_kernel, out_shape=pltpu.VMEM((N_ROWS, TGT, ROWPIECE), BF16), compiler_params=params(4)
    )(parts)


MESSAGE = 72
HALF = PIECE // 2


def column_kernel(x_ref, rows_ref, k_ref, out_ref, half):
    for m in range(N_X):
        for q in range(PER):
            c = m * OWN + q * ROWPIECE
            half[:, c:c + ROWPIECE] = rows_ref[(x_ref[0] ^ m) * PER + q]
    sums = [jnp.dot(half[...], k_ref[i], preferred_element_type=F32) for i in range(N_SPLIT)]
    top = functools.reduce(jnp.maximum, [jnp.abs(v) for v in sums])
    top = jnp.max(jnp.maximum(top[:, :HALF], top[:, HALF:]), axis=1, keepdims=True)
    power = jnp.ceil(jnp.log2(jnp.maximum(jnp.broadcast_to(top, (TGT, HALF)), 1e-30)))
    scale = jnp.exp2(15.0 - power)
    line = jnp.concatenate([power] * (HALF // TGT), axis=0).T[:MESSAGE - 2 * TGT]
    for i in range(N_SPLIT):
        out_ref[i, :TGT, :] = sums[i][:, :HALF] * scale
        out_ref[i, TGT:2 * TGT, :] = sums[i][:, HALF:] * scale
        out_ref[i, 2 * TGT:, :] = line


def column_sums(x, rows, kmat):
    return pl.pallas_call(
        column_kernel,
        in_specs=[IN_SMEM] + [IN_VMEM] * 2,
        out_specs=IN_VMEM,
        out_shape=jax.ShapeDtypeStruct((N_SPLIT, MESSAGE, HALF), F32),
        scratch_shapes=[pltpu.VMEM((TGT, N_EP), BF16)],
        compiler_params=params(8),
        cost_estimate=pl.CostEstimate(flops=2 * TGT * 2 ** 23, bytes_accessed=2 ** 24, transcendentals=0),
    )(x, rows, here(kmat))


def gathered(parts_ref):
    low = high = 0.0
    for i in range(N_SPLIT):
        power = jnp.broadcast_to(parts_ref[i, 2 * TGT:2 * TGT + 1, :], (HALF, HALF)).T[:TGT]
        back = jnp.exp2(power - 15.0)
        low = low + parts_ref[i, :TGT, :] * back
        high = high + parts_ref[i, TGT:2 * TGT, :] * back
    return jnp.concatenate([low, high], axis=1)


def lane_sums(v):
    return jnp.broadcast_to(jnp.sum(v, axis=1, keepdims=True), (TGT, 128))


def wide(v):
    return jnp.concatenate([v, v], axis=1)


def apply_kernel(parts_ref, r_ref, d_ref, applied_ref, sums_ref):
    r, d = r_ref[...], d_ref[...]
    a = gathered(parts_ref) + 1.0 * d
    applied_ref[...] = a
    aa = lane_sums(a * a)
    fit = jnp.where(aa > 0.0, lane_sums(r * a) / jnp.where(aa > 0.0, aa, 1.0), 0.0)
    rest = r - wide(fit) * a
    cols = jnp.concatenate([lane_sums(rest * rest), fit, aa, lane_sums(d * a)], axis=0)
    sums_ref[...] = jnp.broadcast_to(cols.T[:1], sums_ref.shape)


def apply_and_sum(parts, residual, direction):
    return pl.pallas_call(
        apply_kernel,
        out_shape=(pltpu.VMEM((TGT, PIECE), F32), jax.ShapeDtypeStruct((256, 4 * TGT), F32)),
        compiler_params=params(4),
    )(parts, residual, direction)


def step_kernel(sums_ref, coeffs_ref, r_ref, d_ref, a_ref, co_ref, ro_ref, do_ref):
    rest, fit, aa, da = (sums_ref[:, k * TGT:(k + 1) * TGT] for k in range(4))
    old = jnp.sum(rest + fit * (fit * aa), axis=0, keepdims=True)
    step = old / jnp.sum(da, axis=0, keepdims=True)
    off = step - fit
    new = jnp.sum(rest + off * (off * aa), axis=0, keepdims=True)
    step = wide(jnp.broadcast_to(step, (128, TGT)).T)
    beta = wide(jnp.broadcast_to(new / old, (128, TGT)).T)
    d = d_ref[...]
    co_ref[...] = coeffs_ref[...] + step * d
    res = r_ref[...] - step * a_ref[...]
    ro_ref[...] = res
    do_ref[...] = res + beta * d


def step_and_update(sums, coeffs, residual, direction, applied):
    return pl.pallas_call(
        step_kernel,
        out_shape=(jax.ShapeDtypeStruct((TGT, PIECE), F32),) * 3,
        compiler_params=params(4),
    )(sums, coeffs, residual, direction, here(applied))


def from_x(v, m):
    return lax.ppermute(v, "x", [(k, k ^ m) for k in range(N_X)])


def shards(episodes, centers, coeffs, residual, direction):
    x = lax.axis_index("x").reshape(1)
    near = from_x(episodes, 1)
    far = from_x(near, 3), from_x(near, 2)
    dirs = exchange(copies(direction), SPLIT)
    early, right = early_tiles(x, episodes, near, centers)
    kmat, row_parts = tiles_and_rows(x, far, right, early, dirs)
    row_parts = exchange(row_parts, ROWS)
    rows = exchange(spread(row_parts), ROWS)
    parts = column_sums(x, rows, kmat).astype(F16)
    parts = lax.all_to_all(parts, SPLIT, 0, 0, tiled=False).astype(F32)
    applied, sums = apply_and_sum(parts, residual, direction)
    sums = lax.all_to_all(sums.reshape(256, 1, 4 * TGT), AXES, 0, 0, tiled=False).reshape(256, 4 * TGT)
    return step_and_update(sums, coeffs, residual, direction, applied)


def solution(mesh):
    fine = Mesh(mesh.devices.reshape(SIZES), AXES)
    piece = P(None, CTR + EP)
    return jax.shard_map(
        shards,
        mesh=fine,
        in_specs=(P(None, EP), P(None, CTR), piece, piece, piece),
        out_specs=(piece, piece, piece),
        check_vma=False,
    )
```

```python
import functools

import jax
import jax.numpy as jnp
from jax import lax
from jax.experimental import pallas as pl
from jax.experimental.pallas import tpu as pltpu
from jax.sharding import Mesh, PartitionSpec as P

AXES = ("yh", "z", "x", "yl", "c")
SIZES = (2, 8, 4, 2, 2)
EP = ("yh", "z", "x")
CTR = ("yl", "c")
SPLIT = ("yh", "z")
ROWS = ("x", "yl", "c")
N_SPLIT, N_X, N_ROWS = 16, 4, 16

F = 96
DEPTH = 128
TGT = 32
PIECE = 256
ROWPIECE = 128
OWN = 512
PER = OWN // ROWPIECE
N_EP = N_X * OWN
EARLY = 2 * OWN
SHARP = 3.0 / F
F32 = jnp.float32
BF16 = jnp.bfloat16
F16 = jnp.float16
IN_VMEM = pl.BlockSpec(memory_space=pltpu.VMEM)
IN_SMEM = pl.BlockSpec(memory_space=pltpu.SMEM)
ANYWHERE = pl.BlockSpec(memory_space=pl.ANY)


def params(mib):
    return pltpu.CompilerParams(vmem_limit_bytes=mib * 1024 * 1024)


def here(x):
    return pltpu.with_memory_space_constraint(x, pltpu.VMEM)


def in_hbm(x):
    return pltpu.with_memory_space_constraint(x, pltpu.HBM)


def exchange(x, axes):
    return here(lax.all_to_all(here(x), axes, 0, 0, tiled=False))


def three(v):
    hi = v.astype(BF16).astype(F32)
    mid = (v - hi).astype(BF16).astype(F32)
    return hi, mid, v - hi - mid


def extra_rows(norm_parts, first, width):
    row = lax.broadcasted_iota(jnp.int32, (DEPTH - F, width), 0)
    out = jnp.where(row < 6, 1.0, 0.0).astype(F32)
    for k, part in enumerate(norm_parts):
        out = jnp.where(row == first + k, part, out)
    return out


def first_kernel(place_ref, d_ref, e_ref, cen_ref, out_ref, own_ref, cens_ref, mine, sems):
    loads = [pltpu.make_async_copy(d_ref, mine, sems.at[0]), pltpu.make_async_copy(e_ref, own_ref, sems.at[1])]
    for i in range(N_SPLIT):
        start = pl.multiple_of((place_ref[0] + i * N_X) * PIECE, PIECE)
        loads.append(pltpu.make_async_copy(cen_ref.at[:, pl.ds(start, PIECE)], cens_ref.at[i], sems.at[2 + i]))
    for load in loads:
        load.start()
    loads[0].wait()
    half = mine[...].astype(BF16)
    for i in range(N_SPLIT):
        out_ref[i] = half
    for load in loads[1:]:
        load.wait()


def first_copies(place, direction, episodes, centers):
    return pl.pallas_call(
        first_kernel,
        in_specs=[IN_SMEM] + [ANYWHERE] * 3,
        out_specs=(IN_VMEM,) * 3,
        out_shape=(
            pltpu.VMEM((N_SPLIT, TGT, PIECE), BF16),
            pltpu.VMEM((F, OWN), BF16),
            pltpu.VMEM((N_SPLIT, F, PIECE), BF16),
        ),
        scratch_shapes=[pltpu.VMEM((TGT, PIECE), F32), pltpu.SemaphoreType.DMA((2 + N_SPLIT,))],
        compiler_params=params(4),
    )(place, in_hbm(direction), in_hbm(episodes), in_hbm(centers))


def left_block(e):
    e = e.astype(F32)
    norm = jnp.sum(e * e, axis=0, keepdims=True)
    tall = jnp.concatenate([e * (2.0 * SHARP), extra_rows(three(-SHARP * norm), 0, OWN)], axis=0)
    return tall.T.astype(BF16)


def tile(left, right):
    return jnp.exp(jnp.dot(left, right, preferred_element_type=F32)).astype(BF16)


def early_kernel(own_ref, next_ref, cens, k_ref, right_ref, left, ready, out_sems):
    def store(i):
        return pltpu.make_async_copy(ready.at[i], k_ref.at[i], out_sems.at[i])

    left[:OWN, :] = left_block(own_ref[...])
    left[OWN:, :] = left_block(next_ref[...])
    for i in range(N_SPLIT):
        c = cens[i].astype(F32)
        norm = jnp.sum(c * c, axis=0, keepdims=True)
        right = jnp.concatenate([cens[i], extra_rows(three(-SHARP * norm), 3, PIECE).astype(BF16)], axis=0)
        right_ref[i] = right
        for r in range(0, EARLY, 256):
            ready[i, r:r + 256, :] = tile(left[r:r + 256, :], right)
        store(i).start()
    for i in range(N_SPLIT):
        store(i).wait()


def early_tiles(own, near, cens):
    return pl.pallas_call(
        early_kernel,
        in_specs=[IN_VMEM] * 3,
        out_specs=(ANYWHERE, IN_VMEM),
        out_shape=(
            pltpu.HBM((N_SPLIT, EARLY, PIECE), BF16),
            jax.ShapeDtypeStruct((N_SPLIT, DEPTH, PIECE), BF16),
        ),
        scratch_shapes=[
            pltpu.VMEM((EARLY, DEPTH), BF16),
            pltpu.VMEM((N_SPLIT, EARLY, PIECE), BF16),
            pltpu.SemaphoreType.DMA((N_SPLIT,)),
        ],
        compiler_params=params(20),
        cost_estimate=pl.CostEstimate(flops=10 ** 11, bytes_accessed=2 ** 23, transcendentals=2 ** 22),
    )(own, near, cens)


def late_kernel(x_ref, p2_ref, p3_ref, right_ref, early_ref, d_ref, k_ref, out_ref, left, sem):
    load = pltpu.make_async_copy(early_ref, k_ref.at[:, pl.ds(0, EARLY), :], sem)
    load.start()
    for m, ref in enumerate((p2_ref, p3_ref)):
        left[m * OWN:(m + 1) * OWN, :] = left_block(ref[...])
    for i in range(N_SPLIT):
        for r in range(0, N_EP - EARLY, 256):
            k_ref[i, EARLY + r:EARLY + r + 256, :] = tile(left[r:r + 256, :], right_ref[i])
    for m in (2, 3, 0, 1):
        if m == 0:
            load.wait()
        total = None
        for i in range(N_SPLIT):
            part = lax.dot_general(
                k_ref[i, m * OWN:(m + 1) * OWN, :], d_ref[i], (((1,), (1,)), ((), ())), preferred_element_type=F32
            )
            total = part if total is None else total + part
        total = total.T
        for q in range(PER):
            out_ref[(x_ref[0] ^ m) * PER + q] = total[:, q * ROWPIECE:(q + 1) * ROWPIECE]


def tiles_and_rows(x, far, right, early, dirs):
    return pl.pallas_call(
        late_kernel,
        in_specs=[IN_SMEM] + [IN_VMEM] * 3 + [ANYWHERE, IN_VMEM],
        out_specs=(IN_VMEM,) * 2,
        out_shape=(
            pltpu.VMEM((N_SPLIT, N_EP, PIECE), BF16),
            pltpu.VMEM((N_ROWS, TGT, ROWPIECE), F32),
        ),
        scratch_shapes=[pltpu.VMEM((N_EP - EARLY, DEPTH), BF16), pltpu.SemaphoreType.DMA],
        compiler_params=params(16),
        cost_estimate=pl.CostEstimate(
            flops=2 * (DEPTH + TGT) * 2 ** 23, bytes_accessed=2 ** 24, transcendentals=2 ** 23
        ),
    )(x, *far, right, in_hbm(early), dirs)


def spread_kernel(parts_ref, out_ref):
    half = jnp.sum(parts_ref[...], axis=0).astype(BF16)
    for j in range(N_ROWS):
        out_ref[j] = half


def spread(parts):
    return pl.pallas_call(
        spread_kernel, out_shape=pltpu.VMEM((N_ROWS, TGT, ROWPIECE), BF16), compiler_params=params(4)
    )(parts)


MESSAGE = 72
HALF = PIECE // 2


def column_kernel(x_ref, rows_ref, k_ref, out_ref, half):
    for m in range(N_X):
        for q in range(PER):
            c = m * OWN + q * ROWPIECE
            half[:, c:c + ROWPIECE] = rows_ref[(x_ref[0] ^ m) * PER + q]
    sums = [jnp.dot(half[...], k_ref[i], preferred_element_type=F32) for i in range(N_SPLIT)]
    top = functools.reduce(jnp.maximum, [jnp.abs(v) for v in sums])
    top = jnp.max(jnp.maximum(top[:, :HALF], top[:, HALF:]), axis=1, keepdims=True)
    power = jnp.ceil(jnp.log2(jnp.maximum(jnp.broadcast_to(top, (TGT, HALF)), 1e-30)))
    scale = jnp.exp2(15.0 - power)
    line = jnp.concatenate([power] * (HALF // TGT), axis=0).T[:MESSAGE - 2 * TGT]
    for i in range(N_SPLIT):
        out_ref[i, :TGT, :] = sums[i][:, :HALF] * scale
        out_ref[i, TGT:2 * TGT, :] = sums[i][:, HALF:] * scale
        out_ref[i, 2 * TGT:, :] = line


def column_sums(x, rows, kmat):
    return pl.pallas_call(
        column_kernel,
        in_specs=[IN_SMEM] + [IN_VMEM] * 2,
        out_specs=IN_VMEM,
        out_shape=jax.ShapeDtypeStruct((N_SPLIT, MESSAGE, HALF), F32),
        scratch_shapes=[pltpu.VMEM((TGT, N_EP), BF16)],
        compiler_params=params(8),
        cost_estimate=pl.CostEstimate(flops=2 * TGT * 2 ** 23, bytes_accessed=2 ** 24, transcendentals=0),
    )(x, rows, here(kmat))


def gathered(parts_ref):
    low = high = 0.0
    for i in range(N_SPLIT):
        power = jnp.broadcast_to(parts_ref[i, 2 * TGT:2 * TGT + 1, :], (HALF, HALF)).T[:TGT]
        back = jnp.exp2(power - 15.0)
        low = low + parts_ref[i, :TGT, :] * back
        high = high + parts_ref[i, TGT:2 * TGT, :] * back
    return jnp.concatenate([low, high], axis=1)


def lane_sums(v):
    return jnp.broadcast_to(jnp.sum(v, axis=1, keepdims=True), (TGT, 128))


def wide(v):
    return jnp.concatenate([v, v], axis=1)


def apply_kernel(parts_ref, r_ref, d_ref, applied_ref, sums_ref):
    r, d = r_ref[...], d_ref[...]
    a = gathered(parts_ref) + 1.0 * d
    applied_ref[...] = a
    aa = lane_sums(a * a)
    fit = jnp.where(aa > 0.0, lane_sums(r * a) / jnp.where(aa > 0.0, aa, 1.0), 0.0)
    rest = r - wide(fit) * a
    cols = jnp.concatenate([lane_sums(rest * rest), fit, aa, lane_sums(d * a)], axis=0)
    sums_ref[...] = jnp.broadcast_to(cols.T[:1], sums_ref.shape)


def apply_and_sum(parts, residual, direction):
    return pl.pallas_call(
        apply_kernel,
        out_shape=(pltpu.VMEM((TGT, PIECE), F32), jax.ShapeDtypeStruct((256, 4 * TGT), F32)),
        compiler_params=params(4),
    )(parts, residual, direction)


def step_kernel(sums_ref, coeffs_ref, r_ref, d_ref, a_ref, co_ref, ro_ref, do_ref):
    rest, fit, aa, da = (sums_ref[:, k * TGT:(k + 1) * TGT] for k in range(4))
    old = jnp.sum(rest + fit * (fit * aa), axis=0, keepdims=True)
    step = old / jnp.sum(da, axis=0, keepdims=True)
    off = step - fit
    new = jnp.sum(rest + off * (off * aa), axis=0, keepdims=True)
    step = wide(jnp.broadcast_to(step, (128, TGT)).T)
    beta = wide(jnp.broadcast_to(new / old, (128, TGT)).T)
    d = d_ref[...]
    co_ref[...] = coeffs_ref[...] + step * d
    res = r_ref[...] - step * a_ref[...]
    ro_ref[...] = res
    do_ref[...] = res + beta * d


def step_and_update(sums, coeffs, residual, direction, applied):
    return pl.pallas_call(
        step_kernel,
        out_shape=(jax.ShapeDtypeStruct((TGT, PIECE), F32),) * 3,
        compiler_params=params(4),
    )(sums, coeffs, residual, direction, here(applied))


def from_x(v, m):
    return lax.ppermute(v, "x", [(k, k ^ m) for k in range(N_X)])


def shards(episodes, centers, coeffs, residual, direction):
    x = lax.axis_index("x").reshape(1)
    dirs, own, cens = first_copies(x, direction, episodes, centers)
    near = from_x(own, 1)
    far = from_x(near, 3), from_x(near, 2)
    dirs = exchange(dirs, SPLIT)
    early, right = early_tiles(own, near, cens)
    kmat, row_parts = tiles_and_rows(x, far, right, early, dirs)
    row_parts = exchange(row_parts, ROWS)
    rows = exchange(spread(row_parts), ROWS)
    parts = column_sums(x, rows, kmat).astype(F16)
    parts = lax.all_to_all(parts, SPLIT, 0, 0, tiled=False).astype(F32)
    applied, sums = apply_and_sum(parts, residual, direction)
    sums = lax.all_to_all(sums.reshape(256, 1, 4 * TGT), AXES, 0, 0, tiled=False).reshape(256, 4 * TGT)
    return step_and_update(sums, coeffs, residual, direction, applied)


def solution(mesh):
    fine = Mesh(mesh.devices.reshape(SIZES), AXES)
    piece = P(None, CTR + EP)
    return jax.shard_map(
        shards,
        mesh=fine,
        in_specs=(P(None, EP), P(None, CTR), piece, piece, piece),
        out_specs=(piece, piece, piece),
        check_vma=False,
    )
```

```python
import functools

import jax
import jax.numpy as jnp
from jax import lax
from jax.experimental import pallas as pl
from jax.experimental.pallas import tpu as pltpu
from jax.sharding import Mesh, PartitionSpec as P

AXES = ("yh", "z", "x", "yl", "c")
SIZES = (2, 8, 4, 2, 2)
EP = ("yh", "z", "x")
CTR = ("yl", "c")
SPLIT = ("yh", "z")
ROWS = ("x", "yl", "c")
N_SPLIT, N_X, N_ROWS = 16, 4, 16

F = 96
DEPTH = 128
TGT = 32
PIECE = 256
ROWPIECE = 128
OWN = 512
PER = OWN // ROWPIECE
N_EP = N_X * OWN
EARLY = 2 * OWN
SHARP = 3.0 / F
F32 = jnp.float32
BF16 = jnp.bfloat16
F16 = jnp.float16
IN_VMEM = pl.BlockSpec(memory_space=pltpu.VMEM)
IN_SMEM = pl.BlockSpec(memory_space=pltpu.SMEM)
ANYWHERE = pl.BlockSpec(memory_space=pl.ANY)


def params(mib):
    return pltpu.CompilerParams(vmem_limit_bytes=mib * 1024 * 1024)


def here(x):
    return pltpu.with_memory_space_constraint(x, pltpu.VMEM)


def in_hbm(x):
    return pltpu.with_memory_space_constraint(x, pltpu.HBM)


def exchange(x, axes):
    return here(lax.all_to_all(here(x), axes, 0, 0, tiled=False))


def three(v):
    hi = v.astype(BF16).astype(F32)
    mid = (v - hi).astype(BF16).astype(F32)
    return hi, mid, v - hi - mid


def extra_rows(norm_parts, first, width):
    row = lax.broadcasted_iota(jnp.int32, (DEPTH - F, width), 0)
    out = jnp.where(row < 6, 1.0, 0.0).astype(F32)
    for k, part in enumerate(norm_parts):
        out = jnp.where(row == first + k, part, out)
    return out


def first_kernel(place_ref, d_ref, e_ref, cen_ref, out_ref, own_ref, cens_ref, mine, sems):
    loads = [pltpu.make_async_copy(d_ref, mine, sems.at[0]), pltpu.make_async_copy(e_ref, own_ref, sems.at[1])]
    for i in range(N_SPLIT):
        start = pl.multiple_of((place_ref[0] + i * N_X) * PIECE, PIECE)
        loads.append(pltpu.make_async_copy(cen_ref.at[:, pl.ds(start, PIECE)], cens_ref.at[i], sems.at[2 + i]))
    for load in loads:
        load.start()
    loads[0].wait()
    half = mine[...].astype(BF16)
    for i in range(N_SPLIT):
        out_ref[i] = half
    for load in loads[1:]:
        load.wait()


def first_copies(place, direction, episodes, centers):
    return pl.pallas_call(
        first_kernel,
        in_specs=[IN_SMEM] + [ANYWHERE] * 3,
        out_specs=(IN_VMEM,) * 3,
        out_shape=(
            pltpu.VMEM((N_SPLIT, TGT, PIECE), BF16),
            pltpu.VMEM((F, OWN), BF16),
            pltpu.VMEM((N_SPLIT, F, PIECE), BF16),
        ),
        scratch_shapes=[pltpu.VMEM((TGT, PIECE), F32), pltpu.SemaphoreType.DMA((2 + N_SPLIT,))],
        compiler_params=params(4),
    )(place, in_hbm(direction), in_hbm(episodes), in_hbm(centers))


def left_block(e):
    e = e.astype(F32)
    norm = jnp.sum(e * e, axis=0, keepdims=True)
    tall = jnp.concatenate([e * (2.0 * SHARP), extra_rows(three(-SHARP * norm), 0, OWN)], axis=0)
    return tall.T.astype(BF16)


def tile(left, right):
    return jnp.exp(jnp.dot(left, right, preferred_element_type=F32)).astype(BF16)


def early_kernel(own_ref, next_ref, cens, k_ref, right_ref, left, ready, out_sems):
    def store(i):
        return pltpu.make_async_copy(ready.at[i], k_ref.at[i], out_sems.at[i])

    left[:OWN, :] = left_block(own_ref[...])
    left[OWN:, :] = left_block(next_ref[...])
    for i in range(N_SPLIT):
        c = cens[i].astype(F32)
        norm = jnp.sum(c * c, axis=0, keepdims=True)
        right = jnp.concatenate([cens[i], extra_rows(three(-SHARP * norm), 3, PIECE).astype(BF16)], axis=0)
        right_ref[i] = right
        for r in range(0, EARLY, 256):
            ready[i, r:r + 256, :] = tile(left[r:r + 256, :], right)
        store(i).start()
    for i in range(N_SPLIT):
        store(i).wait()


def early_tiles(own, near, cens):
    return pl.pallas_call(
        early_kernel,
        in_specs=[IN_VMEM] * 3,
        out_specs=(ANYWHERE, IN_VMEM),
        out_shape=(
            pltpu.HBM((N_SPLIT, EARLY, PIECE), BF16),
            jax.ShapeDtypeStruct((N_SPLIT, DEPTH, PIECE), BF16),
        ),
        scratch_shapes=[
            pltpu.VMEM((EARLY, DEPTH), BF16),
            pltpu.VMEM((N_SPLIT, EARLY, PIECE), BF16),
            pltpu.SemaphoreType.DMA((N_SPLIT,)),
        ],
        compiler_params=params(20),
        cost_estimate=pl.CostEstimate(flops=10 ** 11, bytes_accessed=2 ** 23, transcendentals=2 ** 22),
    )(own, near, cens)


def late_kernel(x_ref, p2_ref, p3_ref, right_ref, early_ref, d_ref, k_ref, out_ref, left, sem):
    load = pltpu.make_async_copy(early_ref, k_ref.at[:, pl.ds(0, EARLY), :], sem)
    load.start()
    for m, ref in enumerate((p2_ref, p3_ref)):
        left[m * OWN:(m + 1) * OWN, :] = left_block(ref[...])
    for i in range(N_SPLIT):
        for r in range(0, N_EP - EARLY, 256):
            k_ref[i, EARLY + r:EARLY + r + 256, :] = tile(left[r:r + 256, :], right_ref[i])
    for m in (2, 3, 0, 1):
        if m == 0:
            load.wait()
        total = None
        for i in range(N_SPLIT):
            part = lax.dot_general(
                k_ref[i, m * OWN:(m + 1) * OWN, :], d_ref[i], (((1,), (1,)), ((), ())), preferred_element_type=F32
            )
            total = part if total is None else total + part
        total = total.T
        for q in range(PER):
            out_ref[(x_ref[0] ^ m) * PER + q] = total[:, q * ROWPIECE:(q + 1) * ROWPIECE]


def tiles_and_rows(x, far, right, early, dirs):
    return pl.pallas_call(
        late_kernel,
        in_specs=[IN_SMEM] + [IN_VMEM] * 3 + [ANYWHERE, IN_VMEM],
        out_specs=(IN_VMEM,) * 2,
        out_shape=(
            pltpu.VMEM((N_SPLIT, N_EP, PIECE), BF16),
            pltpu.VMEM((N_ROWS, TGT, ROWPIECE), F32),
        ),
        scratch_shapes=[pltpu.VMEM((N_EP - EARLY, DEPTH), BF16), pltpu.SemaphoreType.DMA],
        compiler_params=params(16),
        cost_estimate=pl.CostEstimate(
            flops=2 * (DEPTH + TGT) * 2 ** 23, bytes_accessed=2 ** 24, transcendentals=2 ** 23
        ),
    )(x, *far, right, in_hbm(early), dirs)


def spread_kernel(parts_ref, out_ref):
    half = jnp.sum(parts_ref[...], axis=0).astype(BF16)
    for j in range(N_ROWS):
        out_ref[j] = half


def spread(parts):
    return pl.pallas_call(
        spread_kernel, out_shape=pltpu.VMEM((N_ROWS, TGT, ROWPIECE), BF16), compiler_params=params(4)
    )(parts)


MESSAGE = 72
HALF = PIECE // 2


def column_kernel(x_ref, rows_ref, k_ref, out_ref, half):
    for m in range(N_X):
        for q in range(PER):
            c = m * OWN + q * ROWPIECE
            half[:, c:c + ROWPIECE] = rows_ref[(x_ref[0] ^ m) * PER + q]
    sums = [jnp.dot(half[...], k_ref[i], preferred_element_type=F32) for i in range(N_SPLIT)]
    top = functools.reduce(jnp.maximum, [jnp.abs(v) for v in sums])
    top = jnp.max(jnp.maximum(top[:, :HALF], top[:, HALF:]), axis=1, keepdims=True)
    power = jnp.ceil(jnp.log2(jnp.maximum(jnp.broadcast_to(top, (TGT, HALF)), 1e-30)))
    scale = jnp.exp2(15.0 - power)
    line = jnp.concatenate([power] * (HALF // TGT), axis=0).T[:MESSAGE - 2 * TGT]
    for i in range(N_SPLIT):
        out_ref[i, :TGT, :] = sums[i][:, :HALF] * scale
        out_ref[i, TGT:2 * TGT, :] = sums[i][:, HALF:] * scale
        out_ref[i, 2 * TGT:, :] = line


def column_sums(x, rows, kmat):
    return pl.pallas_call(
        column_kernel,
        in_specs=[IN_SMEM] + [IN_VMEM] * 2,
        out_specs=IN_VMEM,
        out_shape=jax.ShapeDtypeStruct((N_SPLIT, MESSAGE, HALF), F32),
        scratch_shapes=[pltpu.VMEM((TGT, N_EP), BF16)],
        compiler_params=params(8),
        cost_estimate=pl.CostEstimate(flops=2 * TGT * 2 ** 23, bytes_accessed=2 ** 24, transcendentals=0),
    )(x, rows, here(kmat))


def gathered(parts_ref):
    low = high = 0.0
    powers = jnp.concatenate([parts_ref[i, 2 * TGT:2 * TGT + 1, :] for i in range(N_SPLIT)], axis=0)
    backs = jnp.exp2(powers - 15.0)
    backs = jnp.concatenate([backs, jnp.zeros((HALF - N_SPLIT, HALF), F32)], axis=0).T[:TGT]
    for i in range(N_SPLIT):
        back = jnp.broadcast_to(backs[:, i:i + 1], (TGT, HALF))
        low = low + parts_ref[i, :TGT, :] * back
        high = high + parts_ref[i, TGT:2 * TGT, :] * back
    return jnp.concatenate([low, high], axis=1)


def lane_sums(v):
    return jnp.broadcast_to(jnp.sum(v, axis=1, keepdims=True), (TGT, 128))


def wide(v):
    return jnp.concatenate([v, v], axis=1)


def apply_kernel(parts_ref, r_ref, d_ref, applied_ref, sums_ref):
    r, d = r_ref[...], d_ref[...]
    a = gathered(parts_ref) + 1.0 * d
    applied_ref[...] = a
    aa = lane_sums(a * a)
    fit = jnp.where(aa > 0.0, lane_sums(r * a) / jnp.where(aa > 0.0, aa, 1.0), 0.0)
    rest = r - wide(fit) * a
    cols = jnp.concatenate([lane_sums(rest * rest), fit, aa, lane_sums(d * a)], axis=0)
    sums_ref[...] = jnp.broadcast_to(cols.T[:1], sums_ref.shape)


def apply_and_sum(parts, residual, direction):
    return pl.pallas_call(
        apply_kernel,
        out_shape=(pltpu.VMEM((TGT, PIECE), F32), jax.ShapeDtypeStruct((256, 4 * TGT), F32)),
        compiler_params=params(4),
    )(parts, residual, direction)


def step_kernel(sums_ref, coeffs_ref, r_ref, d_ref, a_ref, co_ref, ro_ref, do_ref):
    rest, fit, aa, da = (sums_ref[:, k * TGT:(k + 1) * TGT] for k in range(4))
    old = jnp.sum(rest + fit * (fit * aa), axis=0, keepdims=True)
    step = old / jnp.sum(da, axis=0, keepdims=True)
    off = step - fit
    new = jnp.sum(rest + off * (off * aa), axis=0, keepdims=True)
    step = wide(jnp.broadcast_to(step, (128, TGT)).T)
    beta = wide(jnp.broadcast_to(new / old, (128, TGT)).T)
    d = d_ref[...]
    co_ref[...] = coeffs_ref[...] + step * d
    res = r_ref[...] - step * a_ref[...]
    ro_ref[...] = res
    do_ref[...] = res + beta * d


def step_and_update(sums, coeffs, residual, direction, applied):
    return pl.pallas_call(
        step_kernel,
        out_shape=(jax.ShapeDtypeStruct((TGT, PIECE), F32),) * 3,
        compiler_params=params(4),
    )(sums, coeffs, residual, direction, here(applied))


def from_x(v, m):
    return lax.ppermute(v, "x", [(k, k ^ m) for k in range(N_X)])


def shards(episodes, centers, coeffs, residual, direction):
    x = lax.axis_index("x").reshape(1)
    dirs, own, cens = first_copies(x, direction, episodes, centers)
    near = from_x(own, 1)
    far = from_x(near, 3), from_x(own, 3)
    dirs = exchange(dirs, SPLIT)
    early, right = early_tiles(own, near, cens)
    kmat, row_parts = tiles_and_rows(x, far, right, early, dirs)
    row_parts = exchange(row_parts, ROWS)
    rows = exchange(spread(row_parts), ROWS)
    parts = column_sums(x, rows, kmat).astype(F16)
    parts = lax.all_to_all(parts, SPLIT, 0, 0, tiled=False).astype(F32)
    applied, sums = apply_and_sum(parts, residual, direction)
    sums = lax.all_to_all(sums.reshape(256, 1, 4 * TGT), AXES, 0, 0, tiled=False).reshape(256, 4 * TGT)
    return step_and_update(sums, coeffs, residual, direction, applied)


def solution(mesh):
    fine = Mesh(mesh.devices.reshape(SIZES), AXES)
    piece = P(None, CTR + EP)
    return jax.shard_map(
        shards,
        mesh=fine,
        in_specs=(P(None, EP), P(None, CTR), piece, piece, piece),
        out_specs=(piece, piece, piece),
        check_vma=False,
    )
```

```python
import functools

import jax
import jax.numpy as jnp
from jax import lax
from jax.experimental import pallas as pl
from jax.experimental.pallas import tpu as pltpu
from jax.sharding import Mesh, PartitionSpec as P

AXES = ("yh", "z", "x", "yl", "c")
SIZES = (2, 8, 4, 2, 2)
EP = ("yh", "z", "x")
CTR = ("yl", "c")
SPLIT = ("yh", "z")
ROWS = ("x", "yl", "c")
N_SPLIT, N_X, N_ROWS = 16, 4, 16

F = 96
DEPTH = 128
TGT = 32
PIECE = 256
ROWPIECE = 128
OWN = 512
PER = OWN // ROWPIECE
N_EP = N_X * OWN
EARLY = 2 * OWN
SHARP = 3.0 / F
F32 = jnp.float32
BF16 = jnp.bfloat16
F16 = jnp.float16
IN_VMEM = pl.BlockSpec(memory_space=pltpu.VMEM)
IN_SMEM = pl.BlockSpec(memory_space=pltpu.SMEM)
ANYWHERE = pl.BlockSpec(memory_space=pl.ANY)


def params(mib):
    return pltpu.CompilerParams(vmem_limit_bytes=mib * 1024 * 1024)


def here(x):
    return pltpu.with_memory_space_constraint(x, pltpu.VMEM)


def in_hbm(x):
    return pltpu.with_memory_space_constraint(x, pltpu.HBM)


def exchange(x, axes):
    return here(lax.all_to_all(here(x), axes, 0, 0, tiled=False))


def three(v):
    hi = v.astype(BF16).astype(F32)
    mid = (v - hi).astype(BF16).astype(F32)
    return hi, mid, v - hi - mid


def extra_rows(norm_parts, first, width):
    row = lax.broadcasted_iota(jnp.int32, (DEPTH - F, width), 0)
    out = jnp.where(row < 6, 1.0, 0.0).astype(F32)
    for k, part in enumerate(norm_parts):
        out = jnp.where(row == first + k, part, out)
    return out


def first_kernel(place_ref, d_ref, e_ref, cen_ref, out_ref, own_ref, cens_ref, mine, sems):
    loads = [pltpu.make_async_copy(d_ref, mine, sems.at[0]), pltpu.make_async_copy(e_ref, own_ref, sems.at[1])]
    for i in range(N_SPLIT):
        start = pl.multiple_of((place_ref[0] + i * N_X) * PIECE, PIECE)
        loads.append(pltpu.make_async_copy(cen_ref.at[:, pl.ds(start, PIECE)], cens_ref.at[i], sems.at[2 + i]))
    for load in loads:
        load.start()
    loads[0].wait()
    half = mine[...].astype(BF16)
    for i in range(N_SPLIT):
        out_ref[i] = half
    for load in loads[1:]:
        load.wait()


def first_copies(place, direction, episodes, centers):
    return pl.pallas_call(
        first_kernel,
        in_specs=[IN_SMEM] + [ANYWHERE] * 3,
        out_specs=(IN_VMEM,) * 3,
        out_shape=(
            pltpu.VMEM((N_SPLIT, TGT, PIECE), BF16),
            pltpu.VMEM((F, OWN), BF16),
            pltpu.VMEM((N_SPLIT, F, PIECE), BF16),
        ),
        scratch_shapes=[pltpu.VMEM((TGT, PIECE), F32), pltpu.SemaphoreType.DMA((2 + N_SPLIT,))],
        compiler_params=params(4),
    )(place, in_hbm(direction), in_hbm(episodes), in_hbm(centers))


def left_block(e):
    e = e.astype(F32)
    norm = jnp.sum(e * e, axis=0, keepdims=True)
    tall = jnp.concatenate([e * (2.0 * SHARP), extra_rows(three(-SHARP * norm), 0, OWN)], axis=0)
    return tall.T.astype(BF16)


def tile(left, right):
    return jnp.exp(jnp.dot(left, right, preferred_element_type=F32)).astype(BF16)


def early_kernel(own_ref, next_ref, cens, k_ref, right_ref, left, ready, out_sems):
    def store(i):
        return pltpu.make_async_copy(ready.at[i], k_ref.at[i], out_sems.at[i])

    left[:OWN, :] = left_block(own_ref[...])
    left[OWN:, :] = left_block(next_ref[...])
    for i in range(N_SPLIT):
        c = cens[i].astype(F32)
        norm = jnp.sum(c * c, axis=0, keepdims=True)
        right = jnp.concatenate([cens[i], extra_rows(three(-SHARP * norm), 3, PIECE).astype(BF16)], axis=0)
        right_ref[i] = right
        for r in range(0, EARLY, 256):
            ready[i, r:r + 256, :] = tile(left[r:r + 256, :], right)
        store(i).start()
    for i in range(N_SPLIT):
        store(i).wait()


def early_tiles(own, near, cens):
    return pl.pallas_call(
        early_kernel,
        in_specs=[IN_VMEM] * 3,
        out_specs=(ANYWHERE, IN_VMEM),
        out_shape=(
            pltpu.HBM((N_SPLIT, EARLY, PIECE), BF16),
            jax.ShapeDtypeStruct((N_SPLIT, DEPTH, PIECE), BF16),
        ),
        scratch_shapes=[
            pltpu.VMEM((EARLY, DEPTH), BF16),
            pltpu.VMEM((N_SPLIT, EARLY, PIECE), BF16),
            pltpu.SemaphoreType.DMA((N_SPLIT,)),
        ],
        compiler_params=params(20),
        cost_estimate=pl.CostEstimate(flops=10 ** 11, bytes_accessed=2 ** 23, transcendentals=2 ** 22),
    )(own, near, cens)


def late_kernel(x_ref, p2_ref, p3_ref, right_ref, early_ref, d_ref, k_ref, out_ref, left, sem):
    load = pltpu.make_async_copy(early_ref, k_ref.at[:, pl.ds(0, EARLY), :], sem)
    load.start()
    for m, ref in enumerate((p2_ref, p3_ref)):
        left[m * OWN:(m + 1) * OWN, :] = left_block(ref[...])
    for i in range(N_SPLIT):
        for r in range(0, N_EP - EARLY, 256):
            k_ref[i, EARLY + r:EARLY + r + 256, :] = tile(left[r:r + 256, :], right_ref[i])
    for m in (2, 3, 0, 1):
        if m == 0:
            load.wait()
        total = None
        for i in range(N_SPLIT):
            part = lax.dot_general(
                k_ref[i, m * OWN:(m + 1) * OWN, :], d_ref[i], (((1,), (1,)), ((), ())), preferred_element_type=F32
            )
            total = part if total is None else total + part
        total = total.T
        for q in range(PER):
            out_ref[(x_ref[0] ^ m) * PER + q] = total[:, q * ROWPIECE:(q + 1) * ROWPIECE]


def tiles_and_rows(x, far, right, early, dirs):
    return pl.pallas_call(
        late_kernel,
        in_specs=[IN_SMEM] + [IN_VMEM] * 3 + [ANYWHERE, IN_VMEM],
        out_specs=(IN_VMEM,) * 2,
        out_shape=(
            pltpu.VMEM((N_SPLIT, N_EP, PIECE), BF16),
            pltpu.VMEM((N_ROWS, TGT, ROWPIECE), F32),
        ),
        scratch_shapes=[pltpu.VMEM((N_EP - EARLY, DEPTH), BF16), pltpu.SemaphoreType.DMA],
        compiler_params=params(16),
        cost_estimate=pl.CostEstimate(
            flops=2 * (DEPTH + TGT) * 2 ** 23, bytes_accessed=2 ** 24, transcendentals=2 ** 23
        ),
    )(x, *far, right, in_hbm(early), dirs)


def spread_kernel(parts_ref, out_ref):
    half = jnp.sum(parts_ref[...], axis=0).astype(BF16)
    for j in range(N_ROWS):
        out_ref[j] = half


def spread(parts):
    return pl.pallas_call(
        spread_kernel, out_shape=pltpu.VMEM((N_ROWS, TGT, ROWPIECE), BF16), compiler_params=params(4)
    )(parts)


MESSAGE = 72
HALF = PIECE // 2


def column_kernel(x_ref, rows_ref, k_ref, out_ref, half):
    for m in range(N_X):
        for q in range(PER):
            c = m * OWN + q * ROWPIECE
            half[:, c:c + ROWPIECE] = rows_ref[(x_ref[0] ^ m) * PER + q]
    sums = [jnp.dot(half[...], k_ref[i], preferred_element_type=F32) for i in range(N_SPLIT)]
    top = functools.reduce(jnp.maximum, [jnp.abs(v) for v in sums])
    top = jnp.max(jnp.maximum(top[:, :HALF], top[:, HALF:]), axis=1, keepdims=True)
    power = jnp.ceil(jnp.log2(jnp.maximum(jnp.broadcast_to(top, (TGT, HALF)), 1e-30)))
    scale = jnp.exp2(15.0 - power)
    line = jnp.concatenate([power] * (HALF // TGT), axis=0).T[:MESSAGE - 2 * TGT]
    for i in range(N_SPLIT):
        out_ref[i, :TGT, :] = sums[i][:, :HALF] * scale
        out_ref[i, TGT:2 * TGT, :] = sums[i][:, HALF:] * scale
        out_ref[i, 2 * TGT:, :] = line


def column_sums(x, rows, kmat):
    return pl.pallas_call(
        column_kernel,
        in_specs=[IN_SMEM] + [IN_VMEM] * 2,
        out_specs=IN_VMEM,
        out_shape=jax.ShapeDtypeStruct((N_SPLIT, MESSAGE, HALF), F32),
        scratch_shapes=[pltpu.VMEM((TGT, N_EP), BF16)],
        compiler_params=params(8),
        cost_estimate=pl.CostEstimate(flops=2 * TGT * 2 ** 23, bytes_accessed=2 ** 24, transcendentals=0),
    )(x, rows, here(kmat))


def gathered(parts_ref):
    low = high = 0.0
    powers = jnp.concatenate([parts_ref[i, 2 * TGT:2 * TGT + 1, :] for i in range(N_SPLIT)], axis=0)
    backs = jnp.exp2(powers - 15.0)
    backs = jnp.concatenate([backs, jnp.zeros((HALF - N_SPLIT, HALF), F32)], axis=0).T[:TGT]
    for i in range(N_SPLIT):
        back = jnp.broadcast_to(backs[:, i:i + 1], (TGT, HALF))
        low = low + parts_ref[i, :TGT, :] * back
        high = high + parts_ref[i, TGT:2 * TGT, :] * back
    return jnp.concatenate([low, high], axis=1)


def lane_sums(v):
    return jnp.broadcast_to(jnp.sum(v, axis=1, keepdims=True), (TGT, 128))


def wide(v):
    return jnp.concatenate([v, v], axis=1)


def apply_kernel(parts_ref, r_ref, d_ref, applied_ref, sums_ref):
    r, d = r_ref[...], d_ref[...]
    a = gathered(parts_ref) + 1.0 * d
    applied_ref[...] = a
    aa = lane_sums(a * a)
    fit = jnp.where(aa > 0.0, lane_sums(r * a) / jnp.where(aa > 0.0, aa, 1.0), 0.0)
    rest = r - wide(fit) * a
    cols = jnp.concatenate([lane_sums(rest * rest), fit, aa, lane_sums(d * a)], axis=0)
    sums_ref[...] = jnp.broadcast_to(cols.T[:1], sums_ref.shape)


def apply_and_sum(parts, residual, direction):
    return pl.pallas_call(
        apply_kernel,
        out_shape=(pltpu.VMEM((TGT, PIECE), F32), jax.ShapeDtypeStruct((256, 4 * TGT), F32)),
        compiler_params=params(4),
    )(parts, residual, direction)


def step_kernel(sums_ref, coeffs_ref, r_ref, d_ref, a_ref, co_ref, ro_ref, do_ref):
    rest, fit, aa, da = (sums_ref[:, k * TGT:(k + 1) * TGT] for k in range(4))
    old = jnp.sum(rest + fit * (fit * aa), axis=0, keepdims=True)
    step = old / jnp.sum(da, axis=0, keepdims=True)
    off = step - fit
    new = jnp.sum(rest + off * (off * aa), axis=0, keepdims=True)
    step = wide(jnp.broadcast_to(step, (128, TGT)).T)
    beta = wide(jnp.broadcast_to(new / old, (128, TGT)).T)
    d = d_ref[...]
    co_ref[...] = coeffs_ref[...] + step * d
    res = r_ref[...] - step * a_ref[...]
    ro_ref[...] = res
    do_ref[...] = res + beta * d


def step_and_update(sums, coeffs, residual, direction, applied):
    return pl.pallas_call(
        step_kernel,
        out_shape=(jax.ShapeDtypeStruct((TGT, PIECE), F32),) * 3,
        compiler_params=params(4),
    )(sums, coeffs, residual, direction, here(applied))


def from_x(v, m):
    return lax.ppermute(v, "x", [(k, k ^ m) for k in range(N_X)])


def shards(episodes, centers, coeffs, residual, direction):
    x = lax.axis_index("x").reshape(1)
    dirs, own, cens = first_copies(x, direction, episodes, centers)
    near = from_x(own, 1)
    late_own, late_near = lax.optimization_barrier((own, near))
    far = from_x(late_near, 3), from_x(late_own, 3)
    dirs = exchange(dirs, SPLIT)
    early, right = early_tiles(own, near, cens)
    kmat, row_parts = tiles_and_rows(x, far, right, early, dirs)
    row_parts = exchange(row_parts, ROWS)
    rows = exchange(spread(row_parts), ROWS)
    parts = column_sums(x, rows, kmat).astype(F16)
    parts = lax.all_to_all(parts, SPLIT, 0, 0, tiled=False).astype(F32)
    applied, sums = apply_and_sum(parts, residual, direction)
    sums = lax.all_to_all(sums.reshape(256, 1, 4 * TGT), AXES[::-1], 0, 0, tiled=False).reshape(256, 4 * TGT)
    return step_and_update(sums, coeffs, residual, direction, applied)


def solution(mesh):
    fine = Mesh(mesh.devices.reshape(SIZES), AXES)
    piece = P(None, CTR + EP)
    return jax.shard_map(
        shards,
        mesh=fine,
        in_specs=(P(None, EP), P(None, CTR), piece, piece, piece),
        out_specs=(piece, piece, piece),
        check_vma=False,
    )
```

```python
import functools

import jax
import jax.numpy as jnp
from jax import lax
from jax.experimental import pallas as pl
from jax.experimental.pallas import tpu as pltpu
from jax.sharding import Mesh, PartitionSpec as P

AXES = ("yh", "z", "x", "yl", "c")
SIZES = (2, 8, 4, 2, 2)
EP = ("yh", "z", "x")
CTR = ("yl", "c")
SPLIT = ("yh", "z")
ROWS = ("x", "yl", "c")
N_SPLIT, N_X, N_ROWS = 16, 4, 16

F = 96
DEPTH = 128
TGT = 32
PIECE = 256
ROWPIECE = 128
OWN = 512
PER = OWN // ROWPIECE
N_EP = N_X * OWN
EARLY = 2 * OWN
SHARP = 3.0 / F
F32 = jnp.float32
BF16 = jnp.bfloat16
F16 = jnp.float16
IN_VMEM = pl.BlockSpec(memory_space=pltpu.VMEM)
IN_SMEM = pl.BlockSpec(memory_space=pltpu.SMEM)
ANYWHERE = pl.BlockSpec(memory_space=pl.ANY)


def params(mib):
    return pltpu.CompilerParams(vmem_limit_bytes=mib * 1024 * 1024)


def here(x):
    return pltpu.with_memory_space_constraint(x, pltpu.VMEM)


def in_hbm(x):
    return pltpu.with_memory_space_constraint(x, pltpu.HBM)


def exchange(x, axes):
    return here(lax.all_to_all(here(x), axes, 0, 0, tiled=False))


def three(v):
    hi = v.astype(BF16).astype(F32)
    mid = (v - hi).astype(BF16).astype(F32)
    return hi, mid, v - hi - mid


def extra_rows(norm_parts, first, width):
    row = lax.broadcasted_iota(jnp.int32, (DEPTH - F, width), 0)
    out = jnp.where(row < 6, 1.0, 0.0).astype(F32)
    for k, part in enumerate(norm_parts):
        out = jnp.where(row == first + k, part, out)
    return out


def first_kernel(place_ref, d_ref, e_ref, cen_ref, out_ref, own_ref, cens_ref, mine, sems):
    loads = [pltpu.make_async_copy(d_ref, mine, sems.at[0]), pltpu.make_async_copy(e_ref, own_ref, sems.at[1])]
    for i in range(N_SPLIT):
        start = pl.multiple_of((place_ref[0] + i * N_X) * PIECE, PIECE)
        loads.append(pltpu.make_async_copy(cen_ref.at[:, pl.ds(start, PIECE)], cens_ref.at[i], sems.at[2 + i]))
    for load in loads:
        load.start()
    loads[0].wait()
    half = mine[...].astype(BF16)
    for i in range(N_SPLIT):
        out_ref[i] = half
    for load in loads[1:]:
        load.wait()


def first_copies(place, direction, episodes, centers):
    return pl.pallas_call(
        first_kernel,
        in_specs=[IN_SMEM] + [ANYWHERE] * 3,
        out_specs=(IN_VMEM,) * 3,
        out_shape=(
            pltpu.VMEM((N_SPLIT, TGT, PIECE), BF16),
            pltpu.VMEM((F, OWN), BF16),
            pltpu.VMEM((N_SPLIT, F, PIECE), BF16),
        ),
        scratch_shapes=[pltpu.VMEM((TGT, PIECE), F32), pltpu.SemaphoreType.DMA((2 + N_SPLIT,))],
        compiler_params=params(4),
    )(place, in_hbm(direction), in_hbm(episodes), in_hbm(centers))


def left_block(e):
    e = e.astype(F32)
    norm = jnp.sum(e * e, axis=0, keepdims=True)
    tall = jnp.concatenate([e * (2.0 * SHARP), extra_rows(three(-SHARP * norm), 0, OWN)], axis=0)
    return tall.astype(BF16).T


def tile(left, right):
    return jnp.exp(jnp.dot(left, right, preferred_element_type=F32)).astype(BF16)


def early_kernel(own_ref, next_ref, cens, k_ref, right_ref, left, ready, out_sems):
    def store(i):
        return pltpu.make_async_copy(ready.at[i], k_ref.at[i], out_sems.at[i])

    left[:OWN, :] = left_block(own_ref[...])
    left[OWN:, :] = left_block(next_ref[...])
    for i in range(N_SPLIT):
        c = cens[i].astype(F32)
        norm = jnp.sum(c * c, axis=0, keepdims=True)
        right = jnp.concatenate([cens[i], extra_rows(three(-SHARP * norm), 3, PIECE).astype(BF16)], axis=0)
        right_ref[i] = right
        for r in range(0, EARLY, 256):
            ready[i, r:r + 256, :] = tile(left[r:r + 256, :], right)
        store(i).start()
    for i in range(N_SPLIT):
        store(i).wait()


def early_tiles(own, near, cens):
    return pl.pallas_call(
        early_kernel,
        in_specs=[IN_VMEM] * 3,
        out_specs=(ANYWHERE, IN_VMEM),
        out_shape=(
            pltpu.HBM((N_SPLIT, EARLY, PIECE), BF16),
            jax.ShapeDtypeStruct((N_SPLIT, DEPTH, PIECE), BF16),
        ),
        scratch_shapes=[
            pltpu.VMEM((EARLY, DEPTH), BF16),
            pltpu.VMEM((N_SPLIT, EARLY, PIECE), BF16),
            pltpu.SemaphoreType.DMA((N_SPLIT,)),
        ],
        compiler_params=params(20),
        cost_estimate=pl.CostEstimate(flops=10 ** 11, bytes_accessed=2 ** 23, transcendentals=2 ** 22),
    )(own, near, cens)


def late_kernel(x_ref, p2_ref, p3_ref, right_ref, early_ref, d_ref, k_ref, out_ref, left, sem):
    load = pltpu.make_async_copy(early_ref, k_ref.at[:, pl.ds(0, EARLY), :], sem)
    load.start()
    for m, ref in enumerate((p2_ref, p3_ref)):
        left[m * OWN:(m + 1) * OWN, :] = left_block(ref[...])
    for i in range(N_SPLIT):
        for r in range(0, N_EP - EARLY, 256):
            k_ref[i, EARLY + r:EARLY + r + 256, :] = tile(left[r:r + 256, :], right_ref[i])
    for m in (2, 3, 0, 1):
        if m == 0:
            load.wait()
        total = None
        for i in range(N_SPLIT):
            part = lax.dot_general(
                k_ref[i, m * OWN:(m + 1) * OWN, :], d_ref[i], (((1,), (1,)), ((), ())), preferred_element_type=F32
            )
            total = part if total is None else total + part
        total = total.T
        for q in range(PER):
            out_ref[(x_ref[0] ^ m) * PER + q] = total[:, q * ROWPIECE:(q + 1) * ROWPIECE]


def tiles_and_rows(x, far, right, early, dirs):
    return pl.pallas_call(
        late_kernel,
        in_specs=[IN_SMEM] + [IN_VMEM] * 3 + [ANYWHERE, IN_VMEM],
        out_specs=(IN_VMEM,) * 2,
        out_shape=(
            pltpu.VMEM((N_SPLIT, N_EP, PIECE), BF16),
            pltpu.VMEM((N_ROWS, TGT, ROWPIECE), F32),
        ),
        scratch_shapes=[pltpu.VMEM((N_EP - EARLY, DEPTH), BF16), pltpu.SemaphoreType.DMA],
        compiler_params=params(16),
        cost_estimate=pl.CostEstimate(
            flops=2 * (DEPTH + TGT) * 2 ** 23, bytes_accessed=2 ** 24, transcendentals=2 ** 23
        ),
    )(x, *far, right, in_hbm(early), dirs)


def spread_kernel(parts_ref, out_ref):
    half = jnp.sum(parts_ref[...], axis=0).astype(BF16)
    for j in range(N_ROWS):
        out_ref[j] = half


def spread(parts):
    return pl.pallas_call(
        spread_kernel, out_shape=pltpu.VMEM((N_ROWS, TGT, ROWPIECE), BF16), compiler_params=params(4)
    )(parts)


MESSAGE = 72
HALF = PIECE // 2


def column_kernel(x_ref, rows_ref, k_ref, out_ref, half):
    for m in range(N_X):
        for q in range(PER):
            c = m * OWN + q * ROWPIECE
            half[:, c:c + ROWPIECE] = rows_ref[(x_ref[0] ^ m) * PER + q]
    sums = [jnp.dot(half[...], k_ref[i], preferred_element_type=F32) for i in range(N_SPLIT)]
    top = functools.reduce(jnp.maximum, [jnp.abs(v) for v in sums])
    top = jnp.max(jnp.maximum(top[:, :HALF], top[:, HALF:]), axis=1, keepdims=True)
    power = jnp.ceil(jnp.log2(jnp.maximum(jnp.broadcast_to(top, (TGT, HALF)), 1e-30)))
    scale = jnp.exp2(15.0 - power)
    line = jnp.concatenate([power] * (HALF // TGT), axis=0).T[:MESSAGE - 2 * TGT]
    for i in range(N_SPLIT):
        out_ref[i, :TGT, :] = sums[i][:, :HALF] * scale
        out_ref[i, TGT:2 * TGT, :] = sums[i][:, HALF:] * scale
        out_ref[i, 2 * TGT:, :] = line


def column_sums(x, rows, kmat):
    return pl.pallas_call(
        column_kernel,
        in_specs=[IN_SMEM] + [IN_VMEM] * 2,
        out_specs=IN_VMEM,
        out_shape=jax.ShapeDtypeStruct((N_SPLIT, MESSAGE, HALF), F32),
        scratch_shapes=[pltpu.VMEM((TGT, N_EP), BF16)],
        compiler_params=params(8),
        cost_estimate=pl.CostEstimate(flops=2 * TGT * 2 ** 23, bytes_accessed=2 ** 24, transcendentals=0),
    )(x, rows, here(kmat))


def gathered(parts_ref):
    low = high = 0.0
    powers = jnp.concatenate([parts_ref[i, 2 * TGT:2 * TGT + 1, :] for i in range(N_SPLIT)], axis=0)
    backs = jnp.exp2(powers - 15.0)
    backs = jnp.concatenate([backs, jnp.zeros((HALF - N_SPLIT, HALF), F32)], axis=0).T[:TGT]
    for i in range(N_SPLIT):
        back = jnp.broadcast_to(backs[:, i:i + 1], (TGT, HALF))
        low = low + parts_ref[i, :TGT, :] * back
        high = high + parts_ref[i, TGT:2 * TGT, :] * back
    return jnp.concatenate([low, high], axis=1)


def lane_sums(v):
    return jnp.broadcast_to(jnp.sum(v, axis=1, keepdims=True), (TGT, 128))


def wide(v):
    return jnp.concatenate([v, v], axis=1)


def apply_kernel(parts_ref, r_ref, d_ref, applied_ref, sums_ref):
    r, d = r_ref[...], d_ref[...]
    a = gathered(parts_ref) + 1.0 * d
    applied_ref[...] = a
    aa = lane_sums(a * a)
    fit = jnp.where(aa > 0.0, lane_sums(r * a) / jnp.where(aa > 0.0, aa, 1.0), 0.0)
    rest = r - wide(fit) * a
    cols = jnp.concatenate([lane_sums(rest * rest), fit, aa, lane_sums(d * a)], axis=0)
    sums_ref[...] = jnp.broadcast_to(cols.T[:1], sums_ref.shape)


def apply_and_sum(parts, residual, direction):
    return pl.pallas_call(
        apply_kernel,
        out_shape=(pltpu.VMEM((TGT, PIECE), F32), jax.ShapeDtypeStruct((256, 4 * TGT), F32)),
        compiler_params=params(4),
    )(parts, residual, direction)


def step_kernel(sums_ref, coeffs_ref, r_ref, d_ref, a_ref, co_ref, ro_ref, do_ref):
    rest, fit, aa, da = (sums_ref[:, k * TGT:(k + 1) * TGT] for k in range(4))
    old = jnp.sum(rest + fit * (fit * aa), axis=0, keepdims=True)
    step = old / jnp.sum(da, axis=0, keepdims=True)
    off = step - fit
    new = jnp.sum(rest + off * (off * aa), axis=0, keepdims=True)
    step = wide(jnp.broadcast_to(step, (128, TGT)).T)
    beta = wide(jnp.broadcast_to(new / old, (128, TGT)).T)
    d = d_ref[...]
    co_ref[...] = coeffs_ref[...] + step * d
    res = r_ref[...] - step * a_ref[...]
    ro_ref[...] = res
    do_ref[...] = res + beta * d


def step_and_update(sums, coeffs, residual, direction, applied):
    return pl.pallas_call(
        step_kernel,
        out_shape=(jax.ShapeDtypeStruct((TGT, PIECE), F32),) * 3,
        compiler_params=params(4),
    )(sums, coeffs, residual, direction, here(applied))


def from_x(v, m):
    return lax.ppermute(v, "x", [(k, k ^ m) for k in range(N_X)])


def shards(episodes, centers, coeffs, residual, direction):
    x = lax.axis_index("x").reshape(1)
    dirs, own, cens = first_copies(x, direction, episodes, centers)
    near = from_x(own, 1)
    late_own, late_near = lax.optimization_barrier((own, near))
    far = from_x(late_near, 3), from_x(late_own, 3)
    dirs = exchange(dirs, SPLIT)
    early, right = early_tiles(own, near, cens)
    kmat, row_parts = tiles_and_rows(x, far, right, early, dirs)
    row_parts = exchange(row_parts, ROWS)
    rows = exchange(spread(row_parts), ROWS)
    parts = column_sums(x, rows, kmat).astype(F16)
    parts = lax.all_to_all(parts, SPLIT, 0, 0, tiled=False).astype(F32)
    applied, sums = apply_and_sum(parts, residual, direction)
    sums = lax.all_to_all(sums.reshape(256, 1, 4 * TGT), AXES[::-1], 0, 0, tiled=False).reshape(256, 4 * TGT)
    return step_and_update(sums, coeffs, residual, direction, applied)


def solution(mesh):
    fine = Mesh(mesh.devices.reshape(SIZES), AXES)
    piece = P(None, CTR + EP)
    return jax.shard_map(
        shards,
        mesh=fine,
        in_specs=(P(None, EP), P(None, CTR), piece, piece, piece),
        out_specs=(piece, piece, piece),
        check_vma=False,
    )
```
